512 devices in a mesh: cfg: 2 (over x_hi), seq: 16 (over y, core), req: 16 (over x_lo, z).
Axes of the slice: x: 4 (x_hi: 2, x_lo: 2; x = x_hi * 2 + x_lo), y: 8, z: 8, core: 2. Of those that a mesh axis runs over, the one named last changes fastest.
Arguments:
- qkv: bfloat16 [2, 3, 16, 1024, 2048], P('cfg', None, 'req', 'seq'), may hold values from -4.5 to 4.5
- residual: bfloat16 [2, 16, 1024, 3072], P('cfg', 'req', 'seq'), may hold values from -6 to 6
- out_weight: bfloat16 [2048, 3072], P('req', 'seq'), may hold values from -0.5 to 0.5
- final_weight: bfloat16 [3072, 64], replicated, may hold values from -0.109375 to 0.109375
- modulation: float32 [2, 3, 3072], P('cfg'), may hold values from -3 to 3
- frames: int32 [16, 8], P('req'), may hold values from 33 to 129, as said below
- timestep: int32 [1], replicated, may hold values from 0 to 49
- noisy: float32 [16, 1024, 64], P('req', 'seq', 'cfg'), may hold values from -6 to 6
Outputs:
- clean_estimate: float32 [16, 1024, 64], P('req', 'seq', 'cfg')
The draws below stay inside these ranges and needn't reach their ends.
Inputs may be any that keep to these rules, and one draw needn't show every extreme that they name: Each value is 4 n + 1. In every group one request has 129 frames and, where a group holds three or more requests, another has 33.
All inputs are finite; a program needn't handle non-finite values.
Results may differ from the reference program's by a relative error of at most 0.008.
Values may be sent and summed in bfloat16 or wider, within the bound.
No kernel may reach another device: no remote copies, remote signals or barrier semaphores. Data moves between devices by JAX's collectives and lax.ppermute only.
A program may use at most 64 MiB of HBM per device.

```python
import jax
import jax.numpy as jnp
from jax import lax

D = 3072
HEADS = 16
HD = 128
CHANNELS = 64
STEPS = 50
INNER = 2048
FRAME_TOK = 2
REQS = 8
GROUPS = 16
GROUP_ROWS = 1024


def draw_frames(key, part):
    key = jax.random.fold_in(key, 5)
    first_key, second_key = jax.random.split(key)
    levels = jax.random.randint(first_key, (GROUPS, REQS), 8, 33)
    scores = jax.random.randint(second_key, (GROUPS, REQS), 0, 65536) * REQS + jnp.arange(REQS, dtype=jnp.int32)[None, :]
    ranks = jnp.argsort(jnp.argsort(scores, axis=1), axis=1)
    if REQS >= 3:
        levels = jnp.where(ranks == 1, 8, levels)
    levels = jnp.where(ranks == 0, 32, levels)
    return (4 * levels + 1).astype(jnp.int32)


def draw_qkv(key, part):
    key = jax.random.fold_in(key, 11)
    shape = (2, 3, GROUPS, GROUP_ROWS, HEADS * HD)
    full = jnp.clip(jax.random.normal(key, shape, jnp.float32), -4.5, 4.5)
    return full.astype(jnp.bfloat16)


def shard_levels(rng, shape, cuts, smallest, high):
    level, own = 1.0, jax.random.fold_in(rng, 6)
    for dim, parts in cuts:
        draws = jnp.exp(jax.random.uniform(jax.random.fold_in(own, dim), (parts,), jnp.float32, smallest / len(cuts), high / len(cuts)))
        level = level * jnp.repeat(draws, shape[dim] // parts).reshape([-1 if axis == dim else 1 for axis in range(len(shape))])
    return level


def gaussian(rng, extent, deviation, bound, cuts=(), kind=jnp.bfloat16):
    values = jax.random.normal(rng, extent, jnp.float32) * deviation
    if len(cuts) > 0:
        values = shard_levels(rng, extent, cuts, -0.22, 0.18) * values
    return jnp.clip(values, min=-bound, max=bound).astype(kind)


def setup_inputs(seed: int = 0) -> dict:
    seeds = jax.random.split(jax.random.key(seed), 9)
    return {
        "qkv": draw_qkv(jax.random.fold_in(seeds[8], 71), 0),
        "residual": gaussian(seeds[1], (2, GROUPS, GROUP_ROWS, D), 1.0, 6.0, ((0, 2), (1, 16), (2, 16))),
        "out_weight": gaussian(seeds[2], (INNER, D), (INNER // 16) ** -0.5, 0.5, ((0, 16), (1, 16))),
        "final_weight": gaussian(seeds[3], (D, CHANNELS), D ** -0.5, 0.109375),
        "modulation": gaussian(seeds[4], (2, 3, D), 0.5, 3.0, ((0, 2),), jnp.float32),
        "frames": draw_frames(jax.random.fold_in(seeds[8], 71), 0),
        "timestep": jax.random.randint(seeds[6], (1,), 0, 50).astype(jnp.int32),
        "noisy": gaussian(seeds[7], (GROUPS, GROUP_ROWS, CHANNELS), 1.0, 6.0, ((0, 16), (1, 16), (2, 2)), jnp.float32),
    }


negative_fill = -1e+30
guide_scale = 6.0
shift_value = 7.0
norm_eps = 1e-06

def segment_ids(frame_counts, total_rows):
    lengths = ((frame_counts - 1) // 4 + 1) * FRAME_TOK
    span_ends = jnp.cumsum(lengths).astype(jnp.int32)
    positions = jnp.arange(total_rows, dtype=jnp.int32)
    return lax.optimization_barrier(jnp.sum((positions[:, None] >= span_ends[None, :]).astype(jnp.int32), axis=1))

def head_attention(query_rows, key_rows, value_rows, same_request):
    scores = jnp.dot(query_rows, key_rows.T, preferred_element_type=jnp.float32) * HD ** (-0.5)
    scores = jnp.where(same_request, scores, negative_fill)
    largest = lax.optimization_barrier(jnp.max(scores, axis=1, keepdims=True))
    weights = jnp.exp(scores - largest)
    row_total = lax.optimization_barrier(jnp.sum(weights, axis=1, keepdims=True))
    combined = jnp.dot(weights.astype(jnp.bfloat16), value_rows, preferred_element_type=jnp.float32)
    return (combined / row_total).astype(jnp.bfloat16)

def group_prediction(qkv_group, stream_rows, frame_counts, out_weight, final_weight, modulation_row):
    segment_of = segment_ids(frame_counts, GROUP_ROWS)
    same_request = segment_of[:, None] == segment_of[None, :]
    split_heads = qkv_group.reshape(3, GROUP_ROWS, HEADS, HD).transpose(0, 2, 1, 3)
    head_major = lax.map(lambda triple: head_attention(triple[0], triple[1], triple[2], same_request), (split_heads[0], split_heads[1], split_heads[2]))
    attention = head_major.transpose(1, 0, 2).reshape(GROUP_ROWS, INNER)
    attn_out = jnp.dot(attention, out_weight, preferred_element_type=jnp.float32).astype(jnp.bfloat16)
    stream = stream_rows.astype(jnp.float32) + modulation_row[0] * attn_out.astype(jnp.float32)
    row_mean = lax.optimization_barrier(jnp.mean(stream, axis=1, keepdims=True))
    centered = stream - row_mean
    row_var = lax.optimization_barrier(jnp.mean(centered * centered, axis=1, keepdims=True))
    normed = (centered / jnp.sqrt(row_var + norm_eps) * (1.0 + modulation_row[2]) + modulation_row[1]).astype(jnp.bfloat16)
    return jnp.dot(normed, final_weight, preferred_element_type=jnp.float32)

def reference(qkv, residual, out_weight, final_weight, modulation, frames, timestep, noisy):
    predictions = []
    for branch in range(2):

        def one_group(packed):
            return group_prediction(packed[0], packed[1], packed[2], out_weight, final_weight, modulation[branch])
        predictions.append(lax.map(one_group, (qkv[branch].transpose(1, 0, 2, 3), residual[branch], frames)))
    conditional, unconditional = (predictions[0], predictions[1])
    guided = unconditional + guide_scale * (conditional - unconditional)
    progress = 1.0 - timestep[0].astype(jnp.float32) / STEPS
    sigma_now = shift_value * progress / (1.0 + (shift_value - 1.0) * progress)
    return noisy - sigma_now * guided
```

```python
import functools

import jax
import jax.numpy as jnp
import numpy as np
from jax import lax
from jax.experimental import pallas as pl
from jax.experimental.pallas import tpu as pltpu
from jax.sharding import Mesh, PartitionSpec as P

HD = 128
STEPS = 50
FRAME_TOK = 2
GUIDE = 6.0
SHIFT = 7.0
EPS = 1e-06
FILL = -1e30
ROWS = 1024
DEV_ROWS = 64
HALF = 1536
WIDTH = 3072
LOG2E = 1.4426950408889634

NT = (((1,), (1,)), ((), ()))
VMEM = pltpu.VMEM
SMEM = pltpu.SMEM


def spec(space):
    return pl.BlockSpec(memory_space=space)


def pack_kernel(in_ref, out_ref):
    for y in range(8):
        for k in range(2):
            head = 8 * k + y
            out_ref[2 * y + k] = in_ref[:, :, head * HD : (head + 1) * HD]


def pack(own):
    return pl.pallas_call(
        pack_kernel,
        out_shape=jax.ShapeDtypeStruct((16, 3, DEV_ROWS, HD), jnp.bfloat16),
        in_specs=[spec(VMEM)],
        out_specs=spec(VMEM),
        name="pack",
    )(own)


BLOCKS = ((0, 128, 0, 256), (128, 256, 0, 1024), (256, 512, 128, 1024), (512, 768, 128, 1024), (768, 1024, 128, 1024))


def attend_kernel(frames_ref, x_ref, out_ref):
    ends = []
    total = jnp.int32(0)
    for r in range(8):
        total = total + ((frames_ref[r] - 1) // 4 + 1) * FRAME_TOK
        ends.append(total)

    def ids(shape, dim, first):
        place = lax.broadcasted_iota(jnp.int32, shape, dim) + first
        found = jnp.zeros(shape, jnp.int32)
        for end in ends:
            found = found + (place >= end).astype(jnp.int32)
        return found

    scale = HD**-0.5 * LOG2E
    for first, last, low, high in BLOCKS:
        n, m = last - first, high - low
        q = x_ref[first // 64 : last // 64, 0].reshape(n, HD)
        k = x_ref[low // 64 : high // 64, 1].reshape(m, HD)
        v = x_ref[low // 64 : high // 64, 2].reshape(m, HD)
        scores = lax.dot_general(q, k, NT, preferred_element_type=jnp.float32)
        same = ids((n, 1), 0, first) == ids((1, m), 1, low)
        scores = jnp.where(same, scores, FILL)
        largest = jnp.max(scores, axis=1, keepdims=True)
        weights = jnp.exp2((scores - largest) * scale)
        denominator = jnp.sum(weights, axis=1, keepdims=True)
        mixed = jnp.dot(weights.astype(jnp.bfloat16), v, preferred_element_type=jnp.float32)
        result = (mixed / denominator).astype(jnp.bfloat16).reshape(n // 128, 128, HD)
        out_ref[0, first // 128 : last // 128] = result
        out_ref[1, first // 128 : last // 128] = result


def attend(frames, gathered):
    return pl.pallas_call(
        attend_kernel,
        out_shape=jax.ShapeDtypeStruct((2, 8, 128, HD), jnp.bfloat16),
        in_specs=[spec(SMEM), spec(VMEM)],
        out_specs=spec(VMEM),
        compiler_params=pltpu.CompilerParams(vmem_limit_bytes=48 * 2**20),
        cost_estimate=pl.CostEstimate(flops=540_000_000, bytes_accessed=2_000_000, transcendentals=1_000_000),
        name="attend",
    )(frames, gathered)


def project_kernel(where_ref, x_ref, w_ref, keep_ref, send_ref):
    core = where_ref[0]
    x = jnp.concatenate([x_ref[:, h].reshape(256, HD) for h in range(8)], axis=1)
    tile = 512
    for t in range(HALF // tile):
        cols = slice(t * tile, (t + 1) * tile)
        w = jnp.concatenate([w_ref[h, cols] for h in range(8)], axis=1)
        part = lax.dot_general(x, w, NT, preferred_element_type=jnp.float32)
        for b in range(2):
            low = part[b * 128 : b * 128 + 64]
            high = part[b * 128 + 64 : b * 128 + 128]
            keep_ref[b, :, cols] = jnp.where(core == 0, low, high)
            send_ref[b, :, cols] = jnp.where(core == 0, high, low).astype(jnp.bfloat16)


def project(where, x, w):
    return pl.pallas_call(
        project_kernel,
        out_shape=(
            jax.ShapeDtypeStruct((2, DEV_ROWS, HALF), jnp.float32),
            jax.ShapeDtypeStruct((2, DEV_ROWS, HALF), jnp.bfloat16),
        ),
        in_specs=[spec(SMEM), spec(VMEM), spec(VMEM)],
        out_specs=(spec(VMEM), spec(VMEM)),
        compiler_params=pltpu.CompilerParams(vmem_limit_bytes=48 * 2**20),
        cost_estimate=pl.CostEstimate(flops=810_000_000, bytes_accessed=5_000_000, transcendentals=0),
        name="project",
    )(where, x, w)


def norm_kernel(where_ref, keep_ref, came_ref, own_ref, other_ref, mod_ref, r_ref, out_ref, send_ref):
    me = where_ref[1]
    lane = lax.broadcasted_iota(jnp.int32, (DEV_ROWS, 128), 1)
    both = jnp.zeros((DEV_ROWS, 256), jnp.float32)
    extra = jnp.zeros((DEV_ROWS, 128), jnp.float32)
    for b in range(2):
        residual = jnp.where(me == b, own_ref[...].astype(jnp.float32), other_ref[...].astype(jnp.float32))
        attn_out = (keep_ref[b] + came_ref[b].astype(jnp.float32)).astype(jnp.bfloat16).astype(jnp.float32)
        stream = residual + mod_ref[b, 0:1] * attn_out
        mean = jnp.mean(stream, axis=1, keepdims=True)
        centered = stream - mean
        spread = jnp.sum(centered * centered, axis=1, keepdims=True)
        scaled = (centered * (1.0 + mod_ref[b, 2:3])).astype(jnp.bfloat16)
        both = both + lax.dot_general(scaled, r_ref[b], NT, preferred_element_type=jnp.float32)
        extra = jnp.where(lane == 64 + b, mean, extra)
        extra = jnp.where(lane == 66 + b, spread, extra)
    out_ref[...] = both[:, :128] + extra
    send_ref[...] = both[:, 128:] + extra


def norm(where, keep, came, own, other, mod, r):
    return pl.pallas_call(
        norm_kernel,
        out_shape=(
            jax.ShapeDtypeStruct((DEV_ROWS, 128), jnp.float32),
            jax.ShapeDtypeStruct((DEV_ROWS, 128), jnp.float32),
        ),
        in_specs=[spec(SMEM)] + [spec(VMEM)] * 6,
        out_specs=(spec(VMEM), spec(VMEM)),
        compiler_params=pltpu.CompilerParams(vmem_limit_bytes=48 * 2**20),
        name="norm",
    )(where, keep, came, own, other, mod, r)


def flip(array, axis):
    return lax.ppermute(array, axis, [(0, 1), (1, 0)])


def spread_pairs():
    pairs = []
    for c in range(2):
        for y in range(8):
            for k in range(2):
                for l in range(2):
                    source = ((c * 8 + y) * 2 + k) * 2 + l
                    target = (((y // 4) * 8 + (y % 4) * 2 + k) * 2 + l) * 2 + c
                    pairs.append((source, target))
    return pairs


def gather_weight(out_weight):
    block = lax.ppermute(out_weight.T, ("c", "y", "k", "l"), spread_pairs())
    unit = lax.all_gather(block, "y", axis=0, tiled=True)
    return lax.all_gather(unit, "z", axis=0, tiled=False)


def shards(qkv, residual, out_weight, final_weight, modulation, frames, timestep, noisy):
    branch = lax.axis_index("c")
    core = lax.axis_index("k")
    where = jnp.stack([core, branch]).astype(jnp.int32)

    packed = pack(qkv[0, :, 0])
    gathered = lax.all_to_all(packed, ("y", "k"), 0, 0, tiled=True)

    weight = gather_weight(out_weight)

    here = lax.dynamic_slice_in_dim(residual[0, 0], branch * HALF, HALF, 1)
    there = lax.dynamic_slice_in_dim(residual[0, 0], (1 - branch) * HALF, HALF, 1)
    other = flip(there, "c")
    mod_other = flip(modulation[0], "c")
    mod_all = jnp.where(branch == 0, jnp.stack([modulation[0], mod_other]), jnp.stack([mod_other, modulation[0]]))
    mod_half = lax.dynamic_slice_in_dim(mod_all, branch * HALF, HALF, 2)

    fw = final_weight.T
    fw_half = lax.dynamic_slice_in_dim(fw, branch * HALF, HALF, 1)
    fw_mine = lax.dynamic_slice_in_dim(fw_half, branch * 32, 32, 0)
    fw_partner = lax.dynamic_slice_in_dim(fw_half, (1 - branch) * 32, 32, 0)
    empty = jnp.zeros((32, HALF), jnp.bfloat16)
    r = jnp.stack(
        [
            jnp.concatenate([fw_mine, empty, empty, empty, fw_partner, empty, empty, empty]),
            jnp.concatenate([empty, fw_mine, empty, empty, empty, fw_partner, empty, empty]),
        ]
    )
    fw_channels = lax.dynamic_slice_in_dim(fw, branch * 32, 32, 0).astype(jnp.float32)
    scaled_sums = jnp.sum((1.0 + mod_all[:, 2])[:, None, :].reshape(2, 1, 2, HALF) * fw_channels.reshape(1, 32, 2, HALF), axis=3)
    tilt = scaled_sums[:, :, 0] - scaled_sums[:, :, 1]
    offset = jnp.sum(mod_all[:, 1][:, None, :] * fw_channels[None], axis=2)

    heads = attend(frames[0], gathered)
    rows = lax.all_to_all(heads.reshape(16, 128, HD), ("c", "y"), 0, 0, tiled=True)
    keep, send = project(where, rows.reshape(2, 8, 128, HD), weight)
    came = flip(send, "k")
    own_sums, partner_sums = norm(where, keep, came, here, other, mod_half, r)
    came_sums = flip(partner_sums, "c")

    prediction = []
    for b in range(2):
        first_mean = jnp.where(branch == 0, own_sums[:, 64 + b], came_sums[:, 64 + b])
        second_mean = jnp.where(branch == 0, came_sums[:, 64 + b], own_sums[:, 64 + b])
        gap = 0.5 * (first_mean - second_mean)
        var = (own_sums[:, 66 + b] + came_sums[:, 66 + b] + WIDTH * gap * gap) / WIDTH
        part = (own_sums + came_sums)[:, 32 * b : 32 * b + 32]
        prediction.append((part + gap[:, None] * tilt[b]) / jnp.sqrt(var + EPS)[:, None] + offset[b])
    guided = prediction[1] + GUIDE * (prediction[0] - prediction[1])
    progress = 1.0 - timestep[0].astype(jnp.float32) / STEPS
    sigma = SHIFT * progress / (1.0 + (SHIFT - 1.0) * progress)
    return noisy - sigma * guided[None]


def solution(mesh):
    fine = Mesh(mesh.devices.reshape(2, 8, 2, 2, 8), ("c", "y", "k", "l", "z"))
    seq, req = ("y", "k"), ("l", "z")
    return jax.shard_map(
        shards,
        mesh=fine,
        in_specs=(
            P("c", None, req, seq, None),
            P("c", req, seq, None),
            P(req, seq),
            P(),
            P("c", None, None),
            P(req, None),
            P(),
            P(req, seq, "c"),
        ),
        out_specs=P(req, seq, "c"),
        check_vma=False,
    )
```

```python
import functools

import jax
import jax.numpy as jnp
import numpy as np
from jax import lax
from jax.experimental import pallas as pl
from jax.experimental.pallas import tpu as pltpu
from jax.sharding import Mesh, PartitionSpec as P

HD = 128
STEPS = 50
FRAME_TOK = 2
GUIDE = 6.0
SHIFT = 7.0
EPS = 1e-06
FILL = -1e30
ROWS = 1024
DEV_ROWS = 64
HALF = 1536
WIDTH = 3072
LOG2E = 1.4426950408889634

NT = (((1,), (1,)), ((), ()))
VMEM = pltpu.VMEM
SMEM = pltpu.SMEM


def spec(space):
    return pl.BlockSpec(memory_space=space)


def pack_kernel(in_ref, out_ref):
    for y in range(8):
        for k in range(2):
            head = 8 * k + y
            out_ref[2 * y + k] = in_ref[:, :, head * HD : (head + 1) * HD]


def pack(own):
    return pl.pallas_call(
        pack_kernel,
        out_shape=jax.ShapeDtypeStruct((16, 3, DEV_ROWS, HD), jnp.bfloat16),
        in_specs=[spec(VMEM)],
        out_specs=spec(VMEM),
        name="pack",
    )(own)


BLOCKS = ((0, 128, 0, 256), (128, 256, 0, 1024), (256, 512, 128, 1024), (512, 768, 128, 1024), (768, 1024, 128, 1024))


def attend_kernel(frames_ref, x_ref, out_ref):
    ends = []
    total = jnp.int32(0)
    for r in range(8):
        total = total + ((frames_ref[r] - 1) // 4 + 1) * FRAME_TOK
        ends.append(total)

    def ids(shape, dim, first):
        place = lax.broadcasted_iota(jnp.int32, shape, dim) + first
        found = jnp.zeros(shape, jnp.int32)
        for end in ends:
            found = found + (place >= end).astype(jnp.int32)
        return found

    scale = HD**-0.5 * LOG2E
    for first, last, low, high in BLOCKS:
        n, m = last - first, high - low
        q = x_ref[first // 64 : last // 64, 0].reshape(n, HD)
        k = x_ref[low // 64 : high // 64, 1].reshape(m, HD)
        v = x_ref[low // 64 : high // 64, 2].reshape(m, HD)
        scores = lax.dot_general(q, k, NT, preferred_element_type=jnp.float32)
        same = ids((n, 1), 0, first) == ids((1, m), 1, low)
        scores = jnp.where(same, scores, FILL)
        largest = jnp.max(scores, axis=1, keepdims=True)
        weights = jnp.exp2((scores - largest) * scale)
        denominator = jnp.sum(weights, axis=1, keepdims=True)
        mixed = jnp.dot(weights.astype(jnp.bfloat16), v, preferred_element_type=jnp.float32)
        result = (mixed / denominator).astype(jnp.bfloat16).reshape(n // 128, 128, HD)
        out_ref[0, first // 128 : last // 128] = result
        out_ref[1, first // 128 : last // 128] = result


def attend(frames, gathered):
    return pl.pallas_call(
        attend_kernel,
        out_shape=jax.ShapeDtypeStruct((2, 8, 128, HD), jnp.bfloat16),
        in_specs=[spec(SMEM), spec(VMEM)],
        out_specs=spec(VMEM),
        compiler_params=pltpu.CompilerParams(vmem_limit_bytes=48 * 2**20),
        cost_estimate=pl.CostEstimate(flops=540_000_000, bytes_accessed=2_000_000, transcendentals=1_000_000),
        name="attend",
    )(frames, gathered)


def project_kernel(where_ref, x_ref, *refs):
    units, (keep_ref, send_ref) = refs[:9], refs[9:]
    core, y, z = where_ref[0], where_ref[2], where_ref[3]
    heads = [lax.rem(z + d + 8, 8) for d in (0, -1, 1, -2, 2, -3, 3, 4)]
    x = jnp.concatenate([x_ref[:, h].reshape(256, HD) for h in heads], axis=1)
    for t in range(4):
        steps = [lax.bitwise_xor(jnp.int32(2 * t + i), y) for i in range(2)]
        slots = [4 * lax.rem(step, 2) + lax.bitwise_and(step, 2) + step // 4 for step in steps]
        tiles = [
            jnp.concatenate([unit[pl.ds(pl.multiple_of(slot * 192, 64), 192)] for slot in slots], axis=0) for unit in units[:7]
        ]
        last = []
        for slot in slots:
            place = pl.ds(pl.multiple_of(lax.rem(slot, 4) * 192, 64), 192)
            last.append(jnp.where(slot >= 4, units[8][place], units[7][place]))
        tiles.append(jnp.concatenate(last, axis=0))
        w = jnp.concatenate(tiles, axis=1)
        part = lax.dot_general(x, w, NT, preferred_element_type=jnp.float32)
        cols = slice(t * 384, (t + 1) * 384)
        for b in range(2):
            low = part[b * 128 : b * 128 + 64]
            high = part[b * 128 + 64 : b * 128 + 128]
            keep_ref[b, :, cols] = jnp.where(core == 0, low, high)
            send_ref[b, :, cols] = jnp.where(core == 0, high, low).astype(jnp.bfloat16)


def project(where, x, units):
    return pl.pallas_call(
        project_kernel,
        out_shape=(
            jax.ShapeDtypeStruct((2, DEV_ROWS, HALF), jnp.float32),
            jax.ShapeDtypeStruct((2, DEV_ROWS, HALF), jnp.bfloat16),
        ),
        in_specs=[spec(SMEM)] + [spec(VMEM)] * 10,
        out_specs=(spec(VMEM), spec(VMEM)),
        compiler_params=pltpu.CompilerParams(vmem_limit_bytes=48 * 2**20),
        cost_estimate=pl.CostEstimate(flops=810_000_000, bytes_accessed=5_000_000, transcendentals=0),
        name="project",
    )(where, x, *units)


def norm_kernel(where_ref, keep_ref, came_ref, own_ref, other_ref, mod_ref, r_ref, out_ref, send_ref):
    me = where_ref[1]
    lane = lax.broadcasted_iota(jnp.int32, (DEV_ROWS, 128), 1)
    both = jnp.zeros((DEV_ROWS, 256), jnp.float32)
    extra = jnp.zeros((DEV_ROWS, 128), jnp.float32)
    for b in range(2):
        residual = jnp.where(me == b, own_ref[...].astype(jnp.float32), other_ref[...].astype(jnp.float32))
        attn_out = (keep_ref[b] + came_ref[b].astype(jnp.float32)).astype(jnp.bfloat16).astype(jnp.float32)
        stream = residual + mod_ref[b, 0:1] * attn_out
        mean = jnp.mean(stream, axis=1, keepdims=True)
        centered = stream - mean
        spread = jnp.sum(centered * centered, axis=1, keepdims=True)
        scaled = (centered * (1.0 + mod_ref[b, 2:3])).astype(jnp.bfloat16)
        both = both + lax.dot_general(scaled, r_ref[b], NT, preferred_element_type=jnp.float32)
        extra = jnp.where(lane == 64 + b, mean, extra)
        extra = jnp.where(lane == 66 + b, spread, extra)
    out_ref[...] = both[:, :128] + extra
    send_ref[...] = both[:, 128:] + extra


def norm(where, keep, came, own, other, mod, r):
    return pl.pallas_call(
        norm_kernel,
        out_shape=(
            jax.ShapeDtypeStruct((DEV_ROWS, 128), jnp.float32),
            jax.ShapeDtypeStruct((DEV_ROWS, 128), jnp.float32),
        ),
        in_specs=[spec(SMEM)] + [spec(VMEM)] * 6,
        out_specs=(spec(VMEM), spec(VMEM)),
        compiler_params=pltpu.CompilerParams(vmem_limit_bytes=48 * 2**20),
        name="norm",
    )(where, keep, came, own, other, mod, r)


def flip(array, axis):
    return lax.ppermute(array, axis, [(0, 1), (1, 0)])


def spread_pairs():
    pairs = []
    for c in range(2):
        for y in range(8):
            for k in range(2):
                for l in range(2):
                    source = ((c * 8 + y) * 2 + k) * 2 + l
                    target = (((y // 4) * 8 + (y % 4) * 2 + k) * 2 + l) * 2 + c
                    pairs.append((source, target))
    return pairs


def gather_weight(out_weight):
    unit = lax.ppermute(out_weight.T, ("c", "y", "k", "l"), spread_pairs())
    for bit in (4, 2, 1):
        unit = jnp.concatenate([unit, lax.ppermute(unit, "y", [(i, i ^ bit) for i in range(8)])])
    up = [(i, (i + 1) % 8) for i in range(8)]
    down = [(i, (i + 7) % 8) for i in range(8)]
    units = [unit]
    from_below = from_above = unit
    for _ in range(3):
        from_below = lax.ppermute(from_below, "z", up)
        from_above = lax.ppermute(from_above, "z", down)
        units += [from_below, from_above]
    half = HALF // 2
    units.append(lax.ppermute(from_below[:half], "z", up))
    units.append(lax.ppermute(from_above[half:], "z", down))
    return units


def shards(qkv, residual, out_weight, final_weight, modulation, frames, timestep, noisy):
    branch = lax.axis_index("c")
    core = lax.axis_index("k")
    where = jnp.stack([core, branch, lax.axis_index("y"), lax.axis_index("z")]).astype(jnp.int32)

    packed = pack(qkv[0, :, 0])
    gathered = lax.all_to_all(packed, ("y", "k"), 0, 0, tiled=True)

    weight = gather_weight(out_weight)

    here = lax.dynamic_slice_in_dim(residual[0, 0], branch * HALF, HALF, 1)
    there = lax.dynamic_slice_in_dim(residual[0, 0], (1 - branch) * HALF, HALF, 1)
    other = flip(there, "c")
    mod_other = flip(modulation[0], "c")
    mod_all = jnp.where(branch == 0, jnp.stack([modulation[0], mod_other]), jnp.stack([mod_other, modulation[0]]))
    mod_half = lax.dynamic_slice_in_dim(mod_all, branch * HALF, HALF, 2)

    fw = final_weight.T
    fw_half = lax.dynamic_slice_in_dim(fw, branch * HALF, HALF, 1)
    fw_mine = lax.dynamic_slice_in_dim(fw_half, branch * 32, 32, 0)
    fw_partner = lax.dynamic_slice_in_dim(fw_half, (1 - branch) * 32, 32, 0)
    empty = jnp.zeros((32, HALF), jnp.bfloat16)
    r = jnp.stack(
        [
            jnp.concatenate([fw_mine, empty, empty, empty, fw_partner, empty, empty, empty]),
            jnp.concatenate([empty, fw_mine, empty, empty, empty, fw_partner, empty, empty]),
        ]
    )
    fw_channels = lax.dynamic_slice_in_dim(fw, branch * 32, 32, 0).astype(jnp.float32)
    scaled_sums = jnp.sum((1.0 + mod_all[:, 2])[:, None, :].reshape(2, 1, 2, HALF) * fw_channels.reshape(1, 32, 2, HALF), axis=3)
    tilt = scaled_sums[:, :, 0] - scaled_sums[:, :, 1]
    offset = jnp.sum(mod_all[:, 1][:, None, :] * fw_channels[None], axis=2)

    heads = attend(frames[0], gathered)
    rows = lax.all_to_all(heads.reshape(16, 128, HD), ("c", "y"), 0, 0, tiled=True)
    keep, send = project(where, rows.reshape(2, 8, 128, HD), weight)
    came = flip(send, "k")
    own_sums, partner_sums = norm(where, keep, came, here, other, mod_half, r)
    came_sums = flip(partner_sums, "c")

    prediction = []
    for b in range(2):
        first_mean = jnp.where(branch == 0, own_sums[:, 64 + b], came_sums[:, 64 + b])
        second_mean = jnp.where(branch == 0, came_sums[:, 64 + b], own_sums[:, 64 + b])
        gap = 0.5 * (first_mean - second_mean)
        var = (own_sums[:, 66 + b] + came_sums[:, 66 + b] + WIDTH * gap * gap) / WIDTH
        part = (own_sums + came_sums)[:, 32 * b : 32 * b + 32]
        prediction.append((part + gap[:, None] * tilt[b]) / jnp.sqrt(var + EPS)[:, None] + offset[b])
    guided = prediction[1] + GUIDE * (prediction[0] - prediction[1])
    progress = 1.0 - timestep[0].astype(jnp.float32) / STEPS
    sigma = SHIFT * progress / (1.0 + (SHIFT - 1.0) * progress)
    return noisy - sigma * guided[None]


def solution(mesh):
    fine = Mesh(mesh.devices.reshape(2, 8, 2, 2, 8), ("c", "y", "k", "l", "z"))
    seq, req = ("y", "k"), ("l", "z")
    return jax.shard_map(
        shards,
        mesh=fine,
        in_specs=(
            P("c", None, req, seq, None),
            P("c", req, seq, None),
            P(req, seq),
            P(),
            P("c", None, None),
            P(req, None),
            P(),
            P(req, seq, "c"),
        ),
        out_specs=P(req, seq, "c"),
        check_vma=False,
    )
```

```python
import functools

import jax
import jax.numpy as jnp
import numpy as np
from jax import lax
from jax.experimental import pallas as pl
from jax.experimental.pallas import tpu as pltpu
from jax.sharding import Mesh, PartitionSpec as P

HD = 128
STEPS = 50
FRAME_TOK = 2
GUIDE = 6.0
SHIFT = 7.0
EPS = 1e-06
FILL = -1e30
ROWS = 1024
DEV_ROWS = 64
HALF = 1536
WIDTH = 3072
LOG2E = 1.4426950408889634

NT = (((1,), (1,)), ((), ()))
VMEM = pltpu.VMEM
SMEM = pltpu.SMEM


def spec(space):
    return pl.BlockSpec(memory_space=space)


def pack_kernel(in_ref, out_ref):
    for y in range(8):
        for k in range(2):
            head = 8 * k + y
            out_ref[2 * y + k] = in_ref[:, :, head * HD : (head + 1) * HD]


def pack(own):
    return pl.pallas_call(
        pack_kernel,
        out_shape=jax.ShapeDtypeStruct((16, 3, DEV_ROWS, HD), jnp.bfloat16),
        in_specs=[spec(VMEM)],
        out_specs=spec(VMEM),
        name="pack",
    )(own)


BLOCKS = ((0, 128, 0, 256), (128, 256, 0, 1024), (256, 512, 128, 1024), (512, 768, 128, 1024), (768, 1024, 128, 1024))


def attend_kernel(frames_ref, x_ref, out_ref):
    ends = []
    total = jnp.int32(0)
    for r in range(8):
        total = total + ((frames_ref[r] - 1) // 4 + 1) * FRAME_TOK
        ends.append(total)

    def ids(shape, dim, first):
        place = lax.broadcasted_iota(jnp.int32, shape, dim) + first
        found = jnp.zeros(shape, jnp.int32)
        for end in ends:
            found = found + (place >= end).astype(jnp.int32)
        return found

    scale = HD**-0.5 * LOG2E
    for first, last, low, high in BLOCKS:
        n, m = last - first, high - low
        q = x_ref[first // 64 : last // 64, 0].reshape(n, HD)
        k = x_ref[low // 64 : high // 64, 1].reshape(m, HD)
        v = x_ref[low // 64 : high // 64, 2].reshape(m, HD)
        scores = lax.dot_general(q, k, NT, preferred_element_type=jnp.float32)
        same = ids((n, 1), 0, first) == ids((1, m), 1, low)
        scores = jnp.where(same, scores, FILL)
        largest = jnp.max(scores, axis=1, keepdims=True)
        weights = jnp.exp2((scores - largest) * scale)
        denominator = jnp.sum(weights, axis=1, keepdims=True)
        mixed = jnp.dot(weights.astype(jnp.bfloat16), v, preferred_element_type=jnp.float32)
        result = (mixed / denominator).astype(jnp.bfloat16).reshape(n // 128, 128, HD)
        out_ref[0, first // 128 : last // 128] = result
        out_ref[1, first // 128 : last // 128] = result


def attend(frames, gathered):
    return pl.pallas_call(
        attend_kernel,
        out_shape=jax.ShapeDtypeStruct((2, 8, 128, HD), jnp.bfloat16),
        in_specs=[spec(SMEM), spec(VMEM)],
        out_specs=spec(VMEM),
        compiler_params=pltpu.CompilerParams(vmem_limit_bytes=32 * 2**20),
        cost_estimate=pl.CostEstimate(flops=540_000_000, bytes_accessed=2_000_000, transcendentals=1_000_000),
        name="attend",
    )(frames, gathered)


def project_kernel(where_ref, x_ref, w_ref, keep_ref, send_ref):
    core = where_ref[0]
    x = jnp.concatenate([x_ref[:, h].reshape(256, HD) for h in range(8)], axis=1)
    tile = 384
    for t in range(HALF // tile):
        cols = slice(t * tile, (t + 1) * tile)
        w = jnp.concatenate([w_ref[h, cols] for h in range(8)], axis=1)
        part = lax.dot_general(x, w, NT, preferred_element_type=jnp.float32)
        for b in range(2):
            low = part[b * 128 : b * 128 + 64]
            high = part[b * 128 + 64 : b * 128 + 128]
            keep_ref[b, :, cols] = jnp.where(core == 0, low, high)
            send_ref[b, :, cols] = jnp.where(core == 0, high, low).astype(jnp.bfloat16)


def project(where, x, w):
    return pl.pallas_call(
        project_kernel,
        out_shape=(
            jax.ShapeDtypeStruct((2, DEV_ROWS, HALF), jnp.float32),
            jax.ShapeDtypeStruct((2, DEV_ROWS, HALF), jnp.bfloat16),
        ),
        in_specs=[spec(SMEM)] + [spec(VMEM)] * 2,
        out_specs=(spec(VMEM), spec(VMEM)),
        compiler_params=pltpu.CompilerParams(vmem_limit_bytes=24 * 2**20),
        cost_estimate=pl.CostEstimate(flops=810_000_000, bytes_accessed=5_000_000, transcendentals=0),
        name="project",
    )(where, x, w)


def split3(x):
    terms = []
    for _ in range(3):
        terms.append(x.astype(jnp.bfloat16))
        x = x - terms[-1].astype(jnp.float32)
    return terms


def prepare_kernel(where_ref, residual_ref, mod_ref, fw_ref, there_ref, side_ref):
    me = where_ref[1]
    cols = pl.ds(pl.multiple_of((1 - me) * HALF, HD), HALF)
    there_ref[:DEV_ROWS] = residual_ref[:, cols]
    terms = split3(mod_ref[:, cols])
    terms.append(jnp.zeros((7, HALF), jnp.bfloat16))
    there_ref[DEV_ROWS:] = jnp.concatenate([term.astype(jnp.float32) for term in terms]).astype(jnp.bfloat16)
    fw = fw_ref[...].astype(jnp.float32)
    sign = jnp.where(lax.broadcasted_iota(jnp.int32, (1, WIDTH), 1) < HALF, 1.0, -1.0)
    tilt = jnp.sum(fw * ((1.0 + mod_ref[2:3]) * sign), axis=1, keepdims=True)
    offset = jnp.sum(fw * mod_ref[1:2], axis=1, keepdims=True)
    lane = lax.broadcasted_iota(jnp.int32, (64, HD), 1)
    side = jnp.where(lane == 0, tilt, jnp.where(lane == 1, offset, 0.0))
    side_ref[:32] = jnp.where(me == 0, side[:32], side[32:])
    side_ref[32:] = jnp.where(me == 0, side[32:], side[:32])


def prepare(where, residual, mod, fw):
    return pl.pallas_call(
        prepare_kernel,
        out_shape=(
            jax.ShapeDtypeStruct((DEV_ROWS + 16, HALF), jnp.bfloat16),
            jax.ShapeDtypeStruct((64, HD), jnp.float32),
        ),
        in_specs=[spec(SMEM)] + [spec(VMEM)] * 3,
        out_specs=(spec(VMEM), spec(VMEM)),
        compiler_params=pltpu.CompilerParams(vmem_limit_bytes=16 * 2**20),
        name="prepare",
    )(where, residual, mod, fw)


def norm_kernel(where_ref, keep_ref, came_ref, residual_ref, other_ref, mod_ref, fw_ref, side_ref, own_ref, send_ref):
    me = where_ref[1]
    cols = pl.ds(pl.multiple_of(me * HALF, HD), HALF)
    own = residual_ref[:, cols].astype(jnp.float32)
    other = other_ref[:DEV_ROWS].astype(jnp.float32)
    mod_own = mod_ref[:, cols]
    tail = other_ref[DEV_ROWS:].astype(jnp.float32)
    mod_other = tail[0:3] + tail[3:6] + tail[6:9]
    lane = lax.broadcasted_iota(jnp.int32, (DEV_ROWS, HD), 1)
    scaled, stats = [], []
    for b in range(2):
        mod = jnp.where(me == b, mod_own, mod_other)
        attn_out = (keep_ref[b] + came_ref[b].astype(jnp.float32)).astype(jnp.bfloat16).astype(jnp.float32)
        stream = jnp.where(me == b, own, other) + mod[0:1] * attn_out
        mean = jnp.mean(stream, axis=1, keepdims=True)
        centered = stream - mean
        spread = jnp.sum(centered * centered, axis=1, keepdims=True)
        scaled.append((centered * (1.0 + mod[2:3])).astype(jnp.bfloat16))
        stats.append(jnp.where(lane == 0, mean, jnp.where(lane == 1, spread, 0.0)))
    sums = lax.dot_general(fw_ref[:, cols], jnp.concatenate(scaled), NT, preferred_element_type=jnp.float32)
    stats = jnp.concatenate(stats).T[:8]
    own_ref[:32] = jnp.where(me == 0, sums[:32], sums[32:])
    send_ref[:32] = jnp.where(me == 0, sums[32:], sums[:32])
    own_ref[32:40] = stats
    send_ref[32:40] = stats
    own_ref[40:] = side_ref[:32]
    send_ref[40:] = side_ref[32:]


def norm(where, *arrays):
    shape = jax.ShapeDtypeStruct((72, HD), jnp.float32)
    return pl.pallas_call(
        norm_kernel,
        out_shape=(shape, shape),
        in_specs=[spec(SMEM)] + [spec(VMEM)] * 7,
        out_specs=(spec(VMEM), spec(VMEM)),
        compiler_params=pltpu.CompilerParams(vmem_limit_bytes=16 * 2**20),
        name="norm",
    )(where, *arrays)


def finish_kernel(where_ref, time_ref, own_ref, came_ref, noisy_ref, out_ref):
    me = where_ref[1]
    ours = (lax.broadcasted_iota(jnp.int32, (32, HD), 1) < DEV_ROWS) == (me == 0)
    tilt = jnp.where(ours, own_ref[40:, 0:1], came_ref[40:, 0:1])
    offset = jnp.where(ours, own_ref[40:, 1:2], came_ref[40:, 1:2])
    gap = 0.5 * (own_ref[32:33] - came_ref[32:33])
    gap = jnp.where(me == 0, gap, -gap)
    var = (own_ref[33:34] + came_ref[33:34]) / WIDTH + gap * gap
    prediction = (own_ref[:32] + came_ref[:32] + gap * tilt) / jnp.sqrt(var + EPS) + offset
    conditional, unconditional = prediction[:, :DEV_ROWS], pltpu.roll(prediction, DEV_ROWS, 1)[:, :DEV_ROWS]
    guided = unconditional + GUIDE * (conditional - unconditional)
    progress = 1.0 - time_ref[0].astype(jnp.float32) / STEPS
    sigma = SHIFT * progress / (1.0 + (SHIFT - 1.0) * progress)
    out_ref[...] = noisy_ref[...] - sigma * guided


def finish(where, timestep, own, came, noisy):
    return pl.pallas_call(
        finish_kernel,
        out_shape=jax.ShapeDtypeStruct((32, DEV_ROWS), jnp.float32),
        in_specs=[spec(SMEM)] * 2 + [spec(VMEM)] * 3,
        out_specs=spec(VMEM),
        compiler_params=pltpu.CompilerParams(vmem_limit_bytes=16 * 2**20),
        name="finish",
    )(where, timestep, own, came, noisy)


SWAP = [(0, 1), (1, 0)]


def spread_pairs():
    pairs = []
    for c in range(2):
        for y in range(8):
            for k in range(2):
                for l in range(2):
                    source = ((c * 8 + y) * 2 + k) * 2 + l
                    target = (((y // 4) * 8 + (y % 4) * 2 + k) * 2 + l) * 2 + c
                    pairs.append((source, target))
    return pairs


def tie(*arrays):
    return lax.optimization_barrier(arrays)


def shards(qkv, residual, out_weight, final_weight, modulation, frames, timestep, noisy):
    branch = lax.axis_index("c")
    where = jnp.stack([lax.axis_index("k"), branch, lax.axis_index("l")]).astype(jnp.int32)
    fw = final_weight.T

    block = lax.ppermute(out_weight.T, ("c", "y", "k", "l"), spread_pairs())
    packed, block = tie(pack(qkv[0, :, 0]), block)
    unit = lax.all_to_all(jnp.broadcast_to(block, (8, 192, HD)), "y", 0, 0, tiled=True).reshape(HALF, HD)
    weight = lax.all_gather(unit, "z", axis=0, tiled=False)

    gathered = lax.all_to_all(packed, ("y", "k"), 0, 0, tiled=True)
    there, sides = prepare(where, residual[0, 0], modulation[0], fw)
    there, unit = tie(there, unit)
    other = lax.ppermute(there, "c", SWAP)

    gathered, other = tie(gathered, other)
    heads = attend(frames[0], gathered)
    rows = lax.all_to_all(heads.reshape(16, 128, HD), ("c", "y"), 0, 0, tiled=True).reshape(2, 8, 128, HD)
    keep, send = project(where, rows, weight)
    came = lax.ppermute(send, "k", SWAP)
    sums, partner_sums = norm(where, keep, came, residual[0, 0], other, modulation[0], fw, sides)
    came_sums = lax.ppermute(partner_sums, "c", SWAP)
    return finish(where, timestep, sums, came_sums, noisy[0].T).T[None]


def solution(mesh):
    fine = Mesh(mesh.devices.reshape(2, 8, 2, 2, 8), ("c", "y", "k", "l", "z"))
    seq, req = ("y", "k"), ("l", "z")
    return jax.shard_map(
        shards,
        mesh=fine,
        in_specs=(
            P("c", None, req, seq, None),
            P("c", req, seq, None),
            P(req, seq),
            P(),
            P("c", None, None),
            P(req, None),
            P(),
            P(req, seq, "c"),
        ),
        out_specs=P(req, seq, "c"),
        check_vma=False,
    )
```

```python
import functools

import jax
import jax.numpy as jnp
import numpy as np
from jax import lax
from jax.experimental import pallas as pl
from jax.experimental.pallas import tpu as pltpu
from jax.sharding import Mesh, PartitionSpec as P

HD = 128
STEPS = 50
FRAME_TOK = 2
GUIDE = 6.0
SHIFT = 7.0
EPS = 1e-06
FILL = -1e30
ROWS = 1024
DEV_ROWS = 64
HALF = 1536
WIDTH = 3072
LOG2E = 1.4426950408889634

NT = (((1,), (1,)), ((), ()))
VMEM = pltpu.VMEM
SMEM = pltpu.SMEM


def spec(space):
    return pl.BlockSpec(memory_space=space)


def pack_kernel(in_ref, out_ref):
    for y in range(8):
        for k in range(2):
            head = 8 * k + y
            out_ref[2 * y + k] = in_ref[:, :, head * HD : (head + 1) * HD]


def pack(own):
    return pl.pallas_call(
        pack_kernel,
        out_shape=jax.ShapeDtypeStruct((16, 3, DEV_ROWS, HD), jnp.bfloat16),
        in_specs=[spec(VMEM)],
        out_specs=spec(VMEM),
        name="pack",
    )(own)


BLOCKS = ((0, 128, 0, 256), (128, 256, 0, 1024), (256, 512, 128, 1024), (512, 768, 128, 1024), (768, 1024, 128, 1024))


def attend_kernel(frames_ref, x_ref, out_ref):
    ends = []
    total = jnp.int32(0)
    for r in range(8):
        total = total + ((frames_ref[r] - 1) // 4 + 1) * FRAME_TOK
        ends.append(total)

    def ids(shape, dim, first):
        place = lax.broadcasted_iota(jnp.int32, shape, dim) + first
        found = jnp.zeros(shape, jnp.int32)
        for end in ends:
            found = found + (place >= end).astype(jnp.int32)
        return found

    scale = HD**-0.5 * LOG2E
    for first, last, low, high in BLOCKS:
        n, m = last - first, high - low
        q = x_ref[first // 64 : last // 64, 0].reshape(n, HD)
        k = x_ref[low // 64 : high // 64, 1].reshape(m, HD)
        v = x_ref[low // 64 : high // 64, 2].reshape(m, HD)
        scores = lax.dot_general(q, k, NT, preferred_element_type=jnp.float32)
        same = ids((n, 1), 0, first) == ids((1, m), 1, low)
        scores = jnp.where(same, scores, FILL)
        largest = jnp.max(scores, axis=1, keepdims=True)
        weights = jnp.exp2((scores - largest) * scale)
        denominator = jnp.sum(weights, axis=1, keepdims=True)
        mixed = jnp.dot(weights.astype(jnp.bfloat16), v, preferred_element_type=jnp.float32)
        result = (mixed / denominator).astype(jnp.bfloat16).reshape(n // 128, 128, HD)
        out_ref[0, first // 128 : last // 128] = result
        out_ref[1, first // 128 : last // 128] = result


def attend(frames, gathered):
    return pl.pallas_call(
        attend_kernel,
        out_shape=jax.ShapeDtypeStruct((2, 8, 128, HD), jnp.bfloat16),
        in_specs=[spec(SMEM), spec(VMEM)],
        out_specs=spec(VMEM),
        compiler_params=pltpu.CompilerParams(vmem_limit_bytes=32 * 2**20),
        cost_estimate=pl.CostEstimate(flops=540_000_000, bytes_accessed=2_000_000, transcendentals=1_000_000),
        name="attend",
    )(frames, gathered)


def project_kernel(where_ref, x_ref, *refs):
    units, (keep_ref, send_ref, *buffers, arrived) = refs[:4], refs[4:]
    copies = [pltpu.make_async_copy(unit, buffer, arrived.at[i]) for i, (unit, buffer) in enumerate(zip(units, buffers))]
    for copy in copies:
        copy.start()
    core, z = where_ref[0], where_ref[2]
    sign = (2 * lax.rem(z, 2) - 1) * (1 - 2 * core)
    heads = [lax.rem(z + offset * sign + 8, 8) for offset in (0, -1, 1, 2, -2, -3, 3, 4)]
    x = jnp.concatenate([x_ref[:, h].reshape(256, HD) for h in heads], axis=1)
    for copy in copies:
        copy.wait()
    tile = 384
    for t in range(HALF // tile):
        cols = slice(t * tile, (t + 1) * tile)
        w = jnp.concatenate([buffers[i // 2][i % 2, cols] for i in range(8)], axis=1)
        part = lax.dot_general(x, w, NT, preferred_element_type=jnp.float32)
        for b in range(2):
            low = part[b * 128 : b * 128 + 64]
            high = part[b * 128 + 64 : b * 128 + 128]
            keep_ref[b, :, cols] = jnp.where(core == 0, low, high)
            send_ref[b, :, cols] = jnp.where(core == 0, high, low).astype(jnp.bfloat16)


def project(where, x, units):
    return pl.pallas_call(
        project_kernel,
        out_shape=(
            jax.ShapeDtypeStruct((2, DEV_ROWS, HALF), jnp.float32),
            jax.ShapeDtypeStruct((2, DEV_ROWS, HALF), jnp.bfloat16),
        ),
        in_specs=[spec(SMEM), spec(VMEM)] + [spec(pl.ANY)] * 4,
        out_specs=(spec(VMEM), spec(VMEM)),
        scratch_shapes=[VMEM((2, HALF, HD), jnp.bfloat16)] * 4 + [pltpu.SemaphoreType.DMA((4,))],
        compiler_params=pltpu.CompilerParams(vmem_limit_bytes=24 * 2**20),
        cost_estimate=pl.CostEstimate(flops=810_000_000, bytes_accessed=5_000_000, transcendentals=0),
        name="project",
    )(where, x, *units)


def split3(x):
    terms = []
    for _ in range(3):
        terms.append(x.astype(jnp.bfloat16))
        x = x - terms[-1].astype(jnp.float32)
    return terms


def blocks_of(array, branch):
    even, odd = [
        jnp.concatenate([array[:, (2 * i + k) * 192 : (2 * i + k + 1) * 192] for i in range(8)], axis=1) for k in range(2)
    ]
    return jnp.where(branch == 0, even, odd)


def prepare_kernel(where_ref, residual_ref, mod_ref, fw_ref, own_ref, there_ref, mod_half_ref, fw_half_ref, side_ref):
    me = where_ref[1]
    residual = residual_ref[...].astype(jnp.float32)
    own_ref[...] = blocks_of(residual, me).astype(jnp.bfloat16)
    mod_half_ref[...] = blocks_of(mod_ref[...], me)
    fw_half_ref[...] = blocks_of(fw_ref[...].astype(jnp.float32), me).astype(jnp.bfloat16)
    there_ref[:DEV_ROWS] = blocks_of(residual, 1 - me).astype(jnp.bfloat16)
    terms = split3(blocks_of(mod_ref[...], 1 - me))
    terms.append(jnp.zeros((7, HALF), jnp.bfloat16))
    there_ref[DEV_ROWS:] = jnp.concatenate([term.astype(jnp.float32) for term in terms]).astype(jnp.bfloat16)
    fw = fw_ref[...].astype(jnp.float32)
    sign = jnp.where(lax.rem(lax.broadcasted_iota(jnp.int32, (1, WIDTH), 1) // 192, 2) == 0, 1.0, -1.0)
    tilt = jnp.sum(fw * ((1.0 + mod_ref[2:3]) * sign), axis=1, keepdims=True)
    offset = jnp.sum(fw * mod_ref[1:2], axis=1, keepdims=True)
    lane = lax.broadcasted_iota(jnp.int32, (64, HD), 1)
    side = jnp.where(lane == 0, tilt, jnp.where(lane == 1, offset, 0.0))
    side_ref[:32] = jnp.where(me == 0, side[:32], side[32:])
    side_ref[32:] = jnp.where(me == 0, side[32:], side[:32])


def prepare(where, residual, mod, fw):
    return pl.pallas_call(
        prepare_kernel,
        out_shape=(
            jax.ShapeDtypeStruct((DEV_ROWS, HALF), jnp.bfloat16),
            jax.ShapeDtypeStruct((DEV_ROWS + 16, HALF), jnp.bfloat16),
            jax.ShapeDtypeStruct((3, HALF), jnp.float32),
            jax.ShapeDtypeStruct((64, HALF), jnp.bfloat16),
            jax.ShapeDtypeStruct((64, HD), jnp.float32),
        ),
        in_specs=[spec(SMEM)] + [spec(VMEM)] * 3,
        out_specs=(spec(VMEM),) * 5,
        compiler_params=pltpu.CompilerParams(vmem_limit_bytes=16 * 2**20),
        name="prepare",
    )(where, residual, mod, fw)


def norm_kernel(where_ref, keep_ref, came_ref, own_ref, other_ref, mod_ref, fw_ref, side_ref, sums_ref, send_ref):
    me = where_ref[1]
    own = own_ref[...].astype(jnp.float32)
    other = other_ref[:DEV_ROWS].astype(jnp.float32)
    tail = other_ref[DEV_ROWS:].astype(jnp.float32)
    mod_own, mod_other = mod_ref[...], tail[0:3] + tail[3:6] + tail[6:9]
    lane = lax.broadcasted_iota(jnp.int32, (DEV_ROWS, HD), 1)
    scaled, stats = [], []
    for b in range(2):
        mod = jnp.where(me == b, mod_own, mod_other)
        attn_out = (keep_ref[b] + came_ref[b].astype(jnp.float32)).astype(jnp.bfloat16).astype(jnp.float32)
        stream = jnp.where(me == b, own, other) + mod[0:1] * attn_out
        mean = jnp.mean(stream, axis=1, keepdims=True)
        centered = stream - mean
        spread = jnp.sum(centered * centered, axis=1, keepdims=True)
        scaled.append((centered * (1.0 + mod[2:3])).astype(jnp.bfloat16))
        stats.append(jnp.where(lane == 0, mean, jnp.where(lane == 1, spread, 0.0)))
    sums = lax.dot_general(fw_ref[...], jnp.concatenate(scaled), NT, preferred_element_type=jnp.float32)
    stats = jnp.concatenate(stats).T[:8]
    sums_ref[:32] = jnp.where(me == 0, sums[:32], sums[32:])
    send_ref[:32] = jnp.where(me == 0, sums[32:], sums[:32])
    sums_ref[32:40] = stats
    send_ref[32:40] = stats
    sums_ref[40:] = side_ref[:32]
    send_ref[40:] = side_ref[32:]


def norm(where, *arrays):
    shape = jax.ShapeDtypeStruct((72, HD), jnp.float32)
    return pl.pallas_call(
        norm_kernel,
        out_shape=(shape, shape),
        in_specs=[spec(SMEM)] + [spec(VMEM)] * 7,
        out_specs=(spec(VMEM), spec(VMEM)),
        compiler_params=pltpu.CompilerParams(vmem_limit_bytes=16 * 2**20),
        name="norm",
    )(where, *arrays)


def finish_kernel(where_ref, time_ref, own_ref, came_ref, noisy_ref, out_ref):
    me = where_ref[1]
    ours = (lax.broadcasted_iota(jnp.int32, (32, HD), 1) < DEV_ROWS) == (me == 0)
    tilt = jnp.where(ours, own_ref[40:, 0:1], came_ref[40:, 0:1])
    offset = jnp.where(ours, own_ref[40:, 1:2], came_ref[40:, 1:2])
    gap = 0.5 * (own_ref[32:33] - came_ref[32:33])
    gap = jnp.where(me == 0, gap, -gap)
    var = (own_ref[33:34] + came_ref[33:34]) / WIDTH + gap * gap
    prediction = (own_ref[:32] + came_ref[:32] + gap * tilt) / jnp.sqrt(var + EPS) + offset
    conditional, unconditional = prediction[:, :DEV_ROWS], pltpu.roll(prediction, DEV_ROWS, 1)[:, :DEV_ROWS]
    guided = unconditional + GUIDE * (conditional - unconditional)
    progress = 1.0 - time_ref[0].astype(jnp.float32) / STEPS
    sigma = SHIFT * progress / (1.0 + (SHIFT - 1.0) * progress)
    out_ref[...] = noisy_ref[...] - sigma * guided


def finish(where, timestep, own, came, noisy):
    return pl.pallas_call(
        finish_kernel,
        out_shape=jax.ShapeDtypeStruct((32, DEV_ROWS), jnp.float32),
        in_specs=[spec(SMEM)] * 2 + [spec(VMEM)] * 3,
        out_specs=spec(VMEM),
        compiler_params=pltpu.CompilerParams(vmem_limit_bytes=16 * 2**20),
        name="finish",
    )(where, timestep, own, came, noisy)


SWAP = [(0, 1), (1, 0)]
EVEN = [(i, i ^ 1) for i in range(8)]
ODD = [(i, ((i ^ 1) + (2 if i % 2 else -2)) % 8) for i in range(8)]
CORES = [EVEN + [(8 + i, 8 + j) for i, j in ODD], ODD + [(8 + i, 8 + j) for i, j in EVEN]]


def spread_pairs():
    pairs = []
    for c in range(2):
        for k in range(2):
            for l in range(2):
                pairs.append(((c * 2 + k) * 2 + l, (k * 2 + l) * 2 + c))
    return pairs


def tie(*arrays):
    return lax.optimization_barrier(arrays)


def shards(qkv, residual, out_weight, final_weight, modulation, frames, timestep, noisy):
    branch = lax.axis_index("c")
    where = jnp.stack([lax.axis_index("k"), branch, lax.axis_index("z")]).astype(jnp.int32)
    fw = final_weight.T

    block = lax.ppermute(out_weight.T, ("c", "k", "l"), spread_pairs())
    packed, block = tie(pack(qkv[0, :, 0]), block)
    unit = lax.all_to_all(jnp.broadcast_to(block, (8, 192, HD)), "y", 0, 0, tiled=True).reshape(HALF, HD)
    gathered = lax.all_to_all(packed, ("y", "k"), 0, 0, tiled=True)

    residual_rows, _ = tie(residual[0, 0], block)
    own, there, mod_half, fw_half, sides = prepare(where, residual_rows, modulation[0], fw)
    other = lax.ppermute(there, "c", SWAP)
    unit, other = tie(unit, other)

    units = [jnp.stack([unit, lax.ppermute(unit, ("k", "z"), CORES[0])])]
    units.append(lax.ppermute(units[0], ("k", "z"), CORES[1]))
    heads = attend(frames[0], gathered)
    heads, latest = tie(heads, units[1])
    for step in (0, 1):
        latest = lax.ppermute(latest, ("k", "z"), CORES[step])
        units.append(latest)
    rows = lax.all_to_all(heads.reshape(16, 128, HD), ("c", "y"), 0, 0, tiled=True).reshape(2, 8, 128, HD)

    keep, send = project(where, rows, units)
    came = lax.ppermute(send, "k", SWAP)
    sums, partner_sums = norm(where, keep, came, own, other, mod_half, fw_half, sides)
    came_sums = lax.ppermute(partner_sums, "c", SWAP)
    return finish(where, timestep, sums, came_sums, noisy[0].T).T[None]


def solution(mesh):
    fine = Mesh(mesh.devices.reshape(2, 8, 2, 2, 8), ("c", "y", "k", "l", "z"))
    seq, req = ("y", "k"), ("l", "z")
    return jax.shard_map(
        shards,
        mesh=fine,
        in_specs=(
            P("c", None, req, seq, None),
            P("c", req, seq, None),
            P(req, seq),
            P(),
            P("c", None, None),
            P(req, None),
            P(),
            P(req, seq, "c"),
        ),
        out_specs=P(req, seq, "c"),
        check_vma=False,
    )
```

```python
import functools

import jax
import jax.numpy as jnp
import numpy as np
from jax import lax
from jax.experimental import pallas as pl
from jax.experimental.pallas import tpu as pltpu
from jax.sharding import Mesh, PartitionSpec as P

HD = 128
STEPS = 50
FRAME_TOK = 2
GUIDE = 6.0
SHIFT = 7.0
EPS = 1e-06
FILL = -1e30
ROWS = 1024
DEV_ROWS = 64
HALF = 1536
WIDTH = 3072
LOG2E = 1.4426950408889634

NT = (((1,), (1,)), ((), ()))
VMEM = pltpu.VMEM
SMEM = pltpu.SMEM


def spec(space):
    return pl.BlockSpec(memory_space=space)


def pack_kernel(in_ref, out_ref):
    for y in range(8):
        for k in range(2):
            head = 8 * k + y
            out_ref[2 * y + k] = in_ref[:, :, head * HD : (head + 1) * HD]


def pack(own):
    return pl.pallas_call(
        pack_kernel,
        out_shape=jax.ShapeDtypeStruct((16, 3, DEV_ROWS, HD), jnp.bfloat16),
        in_specs=[spec(VMEM)],
        out_specs=spec(VMEM),
        name="pack",
    )(own)


BLOCKS = ((0, 128, 0, 256), (128, 256, 0, 1024), (256, 512, 128, 1024), (512, 768, 128, 1024), (768, 1024, 128, 1024))


def attend_kernel(frames_ref, x_ref, out_ref):
    ends = []
    total = jnp.int32(0)
    for r in range(8):
        total = total + ((frames_ref[r] - 1) // 4 + 1) * FRAME_TOK
        ends.append(total)

    def ids(shape, dim, first):
        place = lax.broadcasted_iota(jnp.int32, shape, dim) + first
        found = jnp.zeros(shape, jnp.int32)
        for end in ends:
            found = found + (place >= end).astype(jnp.int32)
        return found

    scale = HD**-0.5 * LOG2E
    for first, last, low, high in BLOCKS:
        n, m = last - first, high - low
        q = x_ref[first // 64 : last // 64, 0].reshape(n, HD)
        k = x_ref[low // 64 : high // 64, 1].reshape(m, HD)
        v = x_ref[low // 64 : high // 64, 2].reshape(m, HD)
        scores = lax.dot_general(q, k, NT, preferred_element_type=jnp.float32)
        same = ids((n, 1), 0, first) == ids((1, m), 1, low)
        scores = jnp.where(same, scores, FILL)
        largest = jnp.max(scores, axis=1, keepdims=True)
        weights = jnp.exp2((scores - largest) * scale)
        denominator = jnp.sum(weights, axis=1, keepdims=True)
        mixed = jnp.dot(weights.astype(jnp.bfloat16), v, preferred_element_type=jnp.float32)
        result = (mixed / denominator).astype(jnp.bfloat16).reshape(n // 128, 128, HD)
        out_ref[0, first // 128 : last // 128] = result
        out_ref[1, first // 128 : last // 128] = result


def attend(frames, gathered):
    return pl.pallas_call(
        attend_kernel,
        out_shape=jax.ShapeDtypeStruct((2, 8, 128, HD), jnp.bfloat16),
        in_specs=[spec(SMEM), spec(VMEM)],
        out_specs=spec(VMEM),
        compiler_params=pltpu.CompilerParams(vmem_limit_bytes=32 * 2**20),
        cost_estimate=pl.CostEstimate(flops=540_000_000, bytes_accessed=2_000_000, transcendentals=1_000_000),
        name="attend",
    )(frames, gathered)


def project_kernel(where_ref, x_ref, *refs):
    units, (keep_ref, send_ref, *buffers, arrived) = refs[:4], refs[4:]
    copies = [pltpu.make_async_copy(unit, buffer, arrived.at[i]) for i, (unit, buffer) in enumerate(zip(units, buffers))]
    for copy in copies:
        copy.start()
    core, z = where_ref[0], where_ref[2]
    sign = (2 * lax.rem(z, 2) - 1) * (1 - 2 * core)
    heads = [lax.rem(z + offset * sign + 8, 8) for offset in (0, -1, 1, 2, -2, -3, 3, 4)]
    x = jnp.concatenate([x_ref[:, h].reshape(256, HD) for h in heads], axis=1)
    for copy in copies:
        copy.wait()
    tile = 384
    for t in range(HALF // tile):
        cols = slice(t * tile, (t + 1) * tile)
        w = jnp.concatenate([buffers[i // 2][i % 2, cols] for i in range(8)], axis=1)
        part = lax.dot_general(x, w, NT, preferred_element_type=jnp.float32)
        for b in range(2):
            low = part[b * 128 : b * 128 + 64]
            high = part[b * 128 + 64 : b * 128 + 128]
            keep_ref[b, :, cols] = jnp.where(core == 0, low, high)
            send_ref[b, :, cols] = jnp.where(core == 0, high, low).astype(jnp.bfloat16)


def project(where, x, units):
    return pl.pallas_call(
        project_kernel,
        out_shape=(
            jax.ShapeDtypeStruct((2, DEV_ROWS, HALF), jnp.float32),
            jax.ShapeDtypeStruct((2, DEV_ROWS, HALF), jnp.bfloat16),
        ),
        in_specs=[spec(SMEM), spec(VMEM)] + [spec(pl.ANY)] * 4,
        out_specs=(spec(VMEM), spec(VMEM)),
        scratch_shapes=[VMEM((2, HALF, HD), jnp.bfloat16)] * 4 + [pltpu.SemaphoreType.DMA((4,))],
        compiler_params=pltpu.CompilerParams(vmem_limit_bytes=24 * 2**20),
        cost_estimate=pl.CostEstimate(flops=810_000_000, bytes_accessed=5_000_000, transcendentals=0),
        name="project",
    )(where, x, *units)


def split3(x):
    terms = []
    for _ in range(3):
        terms.append(x.astype(jnp.bfloat16))
        x = x - terms[-1].astype(jnp.float32)
    return terms


def blocks_of(array, branch):
    even, odd = [
        jnp.concatenate([array[:, (2 * i + k) * 192 : (2 * i + k + 1) * 192] for i in range(8)], axis=1) for k in range(2)
    ]
    return jnp.where(branch == 0, even, odd)


def prepare_kernel(where_ref, residual_ref, mod_ref, fw_ref, own_ref, there_ref, mod_half_ref, fw_half_ref, side_ref):
    me = where_ref[1]
    residual = residual_ref[...].astype(jnp.float32)
    own_ref[...] = blocks_of(residual, me).astype(jnp.bfloat16)
    mod_half_ref[...] = blocks_of(mod_ref[...], me)
    fw_half_ref[...] = blocks_of(fw_ref[...].astype(jnp.float32), me).astype(jnp.bfloat16)
    there_ref[:DEV_ROWS] = blocks_of(residual, 1 - me).astype(jnp.bfloat16)
    terms = split3(blocks_of(mod_ref[...], 1 - me))
    terms.append(jnp.zeros((7, HALF), jnp.bfloat16))
    there_ref[DEV_ROWS:] = jnp.concatenate([term.astype(jnp.float32) for term in terms]).astype(jnp.bfloat16)
    fw = fw_ref[...].astype(jnp.float32)
    sign = jnp.where(lax.rem(lax.broadcasted_iota(jnp.int32, (1, WIDTH), 1) // 192, 2) == 0, 1.0, -1.0)
    tilt = jnp.sum(fw * ((1.0 + mod_ref[2:3]) * sign), axis=1, keepdims=True)
    offset = jnp.sum(fw * mod_ref[1:2], axis=1, keepdims=True)
    lane = lax.broadcasted_iota(jnp.int32, (64, HD), 1)
    side = jnp.where(lane == 0, tilt, jnp.where(lane == 1, offset, 0.0))
    side_ref[:32] = jnp.where(me == 0, side[:32], side[32:])
    side_ref[32:] = jnp.where(me == 0, side[32:], side[:32])


def prepare(where, residual, mod, fw):
    return pl.pallas_call(
        prepare_kernel,
        out_shape=(
            jax.ShapeDtypeStruct((DEV_ROWS, HALF), jnp.bfloat16),
            jax.ShapeDtypeStruct((DEV_ROWS + 16, HALF), jnp.bfloat16),
            jax.ShapeDtypeStruct((3, HALF), jnp.float32),
            jax.ShapeDtypeStruct((64, HALF), jnp.bfloat16),
            jax.ShapeDtypeStruct((64, HD), jnp.float32),
        ),
        in_specs=[spec(SMEM)] + [spec(VMEM)] * 3,
        out_specs=(spec(VMEM),) * 5,
        compiler_params=pltpu.CompilerParams(vmem_limit_bytes=16 * 2**20),
        name="prepare",
    )(where, residual, mod, fw)


def norm_kernel(where_ref, keep_ref, came_ref, own_ref, other_ref, mod_ref, fw_ref, side_ref, sums_ref, send_ref):
    me = where_ref[1]
    own = own_ref[...].astype(jnp.float32)
    other = other_ref[:DEV_ROWS].astype(jnp.float32)
    tail = other_ref[DEV_ROWS:].astype(jnp.float32)
    mod_own, mod_other = mod_ref[...], tail[0:3] + tail[3:6] + tail[6:9]
    lane = lax.broadcasted_iota(jnp.int32, (DEV_ROWS, HD), 1)
    scaled, stats = [], []
    for b in range(2):
        mod = jnp.where(me == b, mod_own, mod_other)
        attn_out = (keep_ref[b] + came_ref[b].astype(jnp.float32)).astype(jnp.bfloat16).astype(jnp.float32)
        stream = jnp.where(me == b, own, other) + mod[0:1] * attn_out
        mean = jnp.mean(stream, axis=1, keepdims=True)
        centered = stream - mean
        spread = jnp.sum(centered * centered, axis=1, keepdims=True)
        scaled.append((centered * (1.0 + mod[2:3])).astype(jnp.bfloat16))
        stats.append(jnp.where(lane == 0, mean, jnp.where(lane == 1, spread, 0.0)))
    sums = lax.dot_general(fw_ref[...], jnp.concatenate(scaled), NT, preferred_element_type=jnp.float32)
    stats = jnp.concatenate(stats).T[:8]
    sums_ref[:32] = jnp.where(me == 0, sums[:32], sums[32:])
    send_ref[:32] = jnp.where(me == 0, sums[32:], sums[:32])
    sums_ref[32:40] = stats
    send_ref[32:40] = stats
    sums_ref[40:] = side_ref[:32]
    send_ref[40:] = side_ref[32:]


def norm(where, *arrays):
    shape = jax.ShapeDtypeStruct((72, HD), jnp.float32)
    return pl.pallas_call(
        norm_kernel,
        out_shape=(shape, shape),
        in_specs=[spec(SMEM)] + [spec(VMEM)] * 7,
        out_specs=(spec(VMEM), spec(VMEM)),
        compiler_params=pltpu.CompilerParams(vmem_limit_bytes=16 * 2**20),
        name="norm",
    )(where, *arrays)


def finish_kernel(where_ref, time_ref, own_ref, came_ref, noisy_ref, out_ref):
    me = where_ref[1]
    ours = (lax.broadcasted_iota(jnp.int32, (32, HD), 1) < DEV_ROWS) == (me == 0)
    tilt = jnp.where(ours, own_ref[40:, 0:1], came_ref[40:, 0:1])
    offset = jnp.where(ours, own_ref[40:, 1:2], came_ref[40:, 1:2])
    gap = 0.5 * (own_ref[32:33] - came_ref[32:33])
    gap = jnp.where(me == 0, gap, -gap)
    var = (own_ref[33:34] + came_ref[33:34]) / WIDTH + gap * gap
    prediction = (own_ref[:32] + came_ref[:32] + gap * tilt) / jnp.sqrt(var + EPS) + offset
    conditional, unconditional = prediction[:, :DEV_ROWS], pltpu.roll(prediction, DEV_ROWS, 1)[:, :DEV_ROWS]
    guided = unconditional + GUIDE * (conditional - unconditional)
    progress = 1.0 - time_ref[0].astype(jnp.float32) / STEPS
    sigma = SHIFT * progress / (1.0 + (SHIFT - 1.0) * progress)
    out_ref[...] = noisy_ref[...] - sigma * guided


def finish(where, timestep, own, came, noisy):
    return pl.pallas_call(
        finish_kernel,
        out_shape=jax.ShapeDtypeStruct((32, DEV_ROWS), jnp.float32),
        in_specs=[spec(SMEM)] * 2 + [spec(VMEM)] * 3,
        out_specs=spec(VMEM),
        compiler_params=pltpu.CompilerParams(vmem_limit_bytes=16 * 2**20),
        name="finish",
    )(where, timestep, own, came, noisy)


SWAP = [(0, 1), (1, 0)]
EVEN = [(i, i ^ 1) for i in range(8)]
ODD = [(i, ((i ^ 1) + (2 if i % 2 else -2)) % 8) for i in range(8)]
CORES = [EVEN + [(8 + i, 8 + j) for i, j in ODD], ODD + [(8 + i, 8 + j) for i, j in EVEN]]


def spread_pairs():
    pairs = []
    for c in range(2):
        for k in range(2):
            for l in range(2):
                pairs.append(((c * 2 + k) * 2 + l, (k * 2 + l) * 2 + c))
    return pairs


def tie(*arrays):
    return lax.optimization_barrier(arrays)


def shards(qkv, residual, out_weight, final_weight, modulation, frames, timestep, noisy):
    branch = lax.axis_index("c")
    where = jnp.stack([lax.axis_index("k"), branch, lax.axis_index("z")]).astype(jnp.int32)
    fw = final_weight.T

    block = lax.ppermute(out_weight.T, ("c", "k", "l"), spread_pairs())
    packed, block = tie(pack(qkv[0, :, 0]), block)
    unit = lax.all_to_all(jnp.broadcast_to(block, (8, 192, HD)), "y", 0, 0, tiled=True).reshape(HALF, HD)
    gathered = lax.all_to_all(packed, ("y", "k"), 0, 0, tiled=True)

    units = [jnp.stack([unit, lax.ppermute(unit, ("k", "z"), CORES[0])])]
    residual_rows, _ = tie(residual[0, 0], units[0])
    own, there, mod_half, fw_half, sides = prepare(where, residual_rows, modulation[0], fw)
    other = lax.ppermute(there, "c", SWAP)
    units.append(lax.ppermute(units[0], ("k", "z"), CORES[1]))
    units[1], other = tie(units[1], other)
    for step in (0, 1):
        units.append(lax.ppermute(units[-1], ("k", "z"), CORES[step]))

    gathered, _ = tie(gathered, units[0])
    heads = attend(frames[0], gathered)
    rows = lax.all_to_all(heads.reshape(16, 128, HD), ("c", "y"), 0, 0, tiled=True).reshape(2, 8, 128, HD)

    keep, send = project(where, rows, units)
    came = lax.ppermute(send, "k", SWAP)
    sums, partner_sums = norm(where, keep, came, own, other, mod_half, fw_half, sides)
    came_sums = lax.ppermute(partner_sums, "c", SWAP)
    return finish(where, timestep, sums, came_sums, noisy[0].T).T[None]


def solution(mesh):
    fine = Mesh(mesh.devices.reshape(2, 8, 2, 2, 8), ("c", "y", "k", "l", "z"))
    seq, req = ("y", "k"), ("l", "z")
    return jax.shard_map(
        shards,
        mesh=fine,
        in_specs=(
            P("c", None, req, seq, None),
            P("c", req, seq, None),
            P(req, seq),
            P(),
            P("c", None, None),
            P(req, None),
            P(),
            P(req, seq, "c"),
        ),
        out_specs=P(req, seq, "c"),
        check_vma=False,
    )
```

```python
import functools

import jax
import jax.numpy as jnp
import numpy as np
from jax import lax
from jax.experimental import pallas as pl
from jax.experimental.pallas import tpu as pltpu
from jax.sharding import Mesh, PartitionSpec as P

HD = 128
STEPS = 50
FRAME_TOK = 2
GUIDE = 6.0
SHIFT = 7.0
EPS = 1e-06
FILL = -1e30
ROWS = 1024
DEV_ROWS = 64
HALF = 1536
WIDTH = 3072
LOG2E = 1.4426950408889634

NT = (((1,), (1,)), ((), ()))
VMEM = pltpu.VMEM
SMEM = pltpu.SMEM


def spec(space):
    return pl.BlockSpec(memory_space=space)


def pack_kernel(in_ref, out_ref):
    for y in range(8):
        for k in range(2):
            head = 8 * k + y
            out_ref[2 * y + k] = in_ref[:, :, head * HD : (head + 1) * HD]


def pack(own):
    return pl.pallas_call(
        pack_kernel,
        out_shape=jax.ShapeDtypeStruct((16, 3, DEV_ROWS, HD), jnp.bfloat16),
        in_specs=[spec(VMEM)],
        out_specs=spec(VMEM),
        name="pack",
    )(own)


BLOCKS = ((0, 128, 0, 256), (128, 256, 0, 1024), (256, 512, 128, 1024), (512, 768, 128, 1024), (768, 1024, 128, 1024))


def attend_kernel(frames_ref, x_ref, out_ref):
    ends = []
    total = jnp.int32(0)
    for r in range(8):
        total = total + ((frames_ref[r] - 1) // 4 + 1) * FRAME_TOK
        ends.append(total)

    def ids(shape, dim, first):
        place = lax.broadcasted_iota(jnp.int32, shape, dim) + first
        found = jnp.zeros(shape, jnp.int32)
        for end in ends:
            found = found + (place >= end).astype(jnp.int32)
        return found

    scale = HD**-0.5 * LOG2E
    for first, last, low, high in BLOCKS:
        n, m = last - first, high - low
        q = x_ref[first // 64 : last // 64, 0].reshape(n, HD)
        k = x_ref[low // 64 : high // 64, 1].reshape(m, HD)
        v = x_ref[low // 64 : high // 64, 2].reshape(m, HD)
        scores = lax.dot_general(q, k, NT, preferred_element_type=jnp.float32)
        same = ids((n, 1), 0, first) == ids((1, m), 1, low)
        scores = jnp.where(same, scores, FILL)
        largest = jnp.max(scores, axis=1, keepdims=True)
        weights = jnp.exp2((scores - largest) * scale)
        denominator = jnp.sum(weights, axis=1, keepdims=True)
        mixed = jnp.dot(weights.astype(jnp.bfloat16), v, preferred_element_type=jnp.float32)
        result = (mixed / denominator).astype(jnp.bfloat16).reshape(n // 128, 128, HD)
        out_ref[0, first // 128 : last // 128] = result
        out_ref[1, first // 128 : last // 128] = result


def attend(frames, gathered):
    return pl.pallas_call(
        attend_kernel,
        out_shape=jax.ShapeDtypeStruct((2, 8, 128, HD), jnp.bfloat16),
        in_specs=[spec(SMEM), spec(VMEM)],
        out_specs=spec(VMEM),
        compiler_params=pltpu.CompilerParams(vmem_limit_bytes=32 * 2**20),
        cost_estimate=pl.CostEstimate(flops=540_000_000, bytes_accessed=2_000_000, transcendentals=1_000_000),
        name="attend",
    )(frames, gathered)


def project_kernel(where_ref, x_ref, *refs):
    units, (keep_ref, send_ref, *buffers, arrived) = refs[:4], refs[4:]
    copies = [pltpu.make_async_copy(unit, buffer, arrived.at[i]) for i, (unit, buffer) in enumerate(zip(units, buffers))]
    for copy in copies:
        copy.start()
    core, z = where_ref[0], where_ref[2]
    sign = (2 * lax.rem(z, 2) - 1) * (1 - 2 * core)
    heads = [lax.rem(z + offset * sign + 8, 8) for offset in (0, -1, 1, 2, -2, -3, 3, 4)]
    x = jnp.concatenate([x_ref[:, h].reshape(256, HD) for h in heads], axis=1)
    for copy in copies:
        copy.wait()
    tile = 384
    for t in range(HALF // tile):
        cols = slice(t * tile, (t + 1) * tile)
        w = jnp.concatenate([buffers[i // 2][i % 2, cols] for i in range(8)], axis=1)
        part = lax.dot_general(x, w, NT, preferred_element_type=jnp.float32)
        for b in range(2):
            low = part[b * 128 : b * 128 + 64]
            high = part[b * 128 + 64 : b * 128 + 128]
            keep_ref[b, :, cols] = jnp.where(core == 0, low, high)
            send_ref[b, :, cols] = jnp.where(core == 0, high, low).astype(jnp.bfloat16)


def project(where, x, units):
    return pl.pallas_call(
        project_kernel,
        out_shape=(
            jax.ShapeDtypeStruct((2, DEV_ROWS, HALF), jnp.float32),
            jax.ShapeDtypeStruct((2, DEV_ROWS, HALF), jnp.bfloat16),
        ),
        in_specs=[spec(SMEM), spec(VMEM)] + [spec(pl.ANY)] * 4,
        out_specs=(spec(VMEM), spec(VMEM)),
        scratch_shapes=[VMEM((2, HALF, HD), jnp.bfloat16)] * 4 + [pltpu.SemaphoreType.DMA((4,))],
        compiler_params=pltpu.CompilerParams(vmem_limit_bytes=24 * 2**20),
        cost_estimate=pl.CostEstimate(flops=810_000_000, bytes_accessed=5_000_000, transcendentals=0),
        name="project",
    )(where, x, *units)


def split3(x):
    terms = []
    for _ in range(3):
        terms.append(x.astype(jnp.bfloat16))
        x = x - terms[-1].astype(jnp.float32)
    return terms


def blocks_of(array, branch):
    even, odd = [
        jnp.concatenate([array[:, (2 * i + k) * 192 : (2 * i + k + 1) * 192] for i in range(8)], axis=1) for k in range(2)
    ]
    return jnp.where(branch == 0, even, odd)


def prepare_kernel(where_ref, residual_ref, mod_ref, fw_ref, own_ref, there_ref, mod_half_ref, fw_half_ref, side_ref):
    me = where_ref[1]
    residual = residual_ref[...].astype(jnp.float32)
    own_ref[...] = blocks_of(residual, me).astype(jnp.bfloat16)
    mod_half_ref[...] = blocks_of(mod_ref[...], me)
    fw_half_ref[...] = blocks_of(fw_ref[...].astype(jnp.float32), me).astype(jnp.bfloat16)
    there_ref[:DEV_ROWS] = blocks_of(residual, 1 - me).astype(jnp.bfloat16)
    terms = split3(blocks_of(mod_ref[...], 1 - me))
    terms.append(jnp.zeros((7, HALF), jnp.bfloat16))
    there_ref[DEV_ROWS:] = jnp.concatenate([term.astype(jnp.float32) for term in terms]).astype(jnp.bfloat16)
    fw = fw_ref[...].astype(jnp.float32)
    sign = jnp.where(lax.rem(lax.broadcasted_iota(jnp.int32, (1, WIDTH), 1) // 192, 2) == 0, 1.0, -1.0)
    tilt = jnp.sum(fw * ((1.0 + mod_ref[2:3]) * sign), axis=1, keepdims=True)
    offset = jnp.sum(fw * mod_ref[1:2], axis=1, keepdims=True)
    lane = lax.broadcasted_iota(jnp.int32, (64, HD), 1)
    side = jnp.where(lane == 0, tilt, jnp.where(lane == 1, offset, 0.0))
    side_ref[:32] = jnp.where(me == 0, side[:32], side[32:])
    side_ref[32:] = jnp.where(me == 0, side[32:], side[:32])


def prepare(where, residual, mod, fw):
    return pl.pallas_call(
        prepare_kernel,
        out_shape=(
            jax.ShapeDtypeStruct((DEV_ROWS, HALF), jnp.bfloat16),
            jax.ShapeDtypeStruct((DEV_ROWS + 16, HALF), jnp.bfloat16),
            jax.ShapeDtypeStruct((3, HALF), jnp.float32),
            jax.ShapeDtypeStruct((64, HALF), jnp.bfloat16),
            jax.ShapeDtypeStruct((64, HD), jnp.float32),
        ),
        in_specs=[spec(SMEM)] + [spec(VMEM)] * 3,
        out_specs=(spec(VMEM),) * 5,
        compiler_params=pltpu.CompilerParams(vmem_limit_bytes=16 * 2**20),
        name="prepare",
    )(where, residual, mod, fw)


def norm_kernel(where_ref, keep_ref, came_ref, own_ref, other_ref, mod_ref, fw_ref, side_ref, sums_ref, send_ref):
    me = where_ref[1]
    own = own_ref[...].astype(jnp.float32)
    other = other_ref[:DEV_ROWS].astype(jnp.float32)
    tail = other_ref[DEV_ROWS:].astype(jnp.float32)
    mod_own, mod_other = mod_ref[...], tail[0:3] + tail[3:6] + tail[6:9]
    lane = lax.broadcasted_iota(jnp.int32, (DEV_ROWS, HD), 1)
    scaled, stats = [], []
    for b in range(2):
        mod = jnp.where(me == b, mod_own, mod_other)
        attn_out = (keep_ref[b] + came_ref[b].astype(jnp.float32)).astype(jnp.bfloat16).astype(jnp.float32)
        stream = jnp.where(me == b, own, other) + mod[0:1] * attn_out
        mean = jnp.mean(stream, axis=1, keepdims=True)
        centered = stream - mean
        spread = jnp.sum(centered * centered, axis=1, keepdims=True)
        scaled.append((centered * (1.0 + mod[2:3])).astype(jnp.bfloat16))
        stats.append(jnp.where(lane == 0, mean, jnp.where(lane == 1, spread, 0.0)))
    sums = lax.dot_general(fw_ref[...], jnp.concatenate(scaled), NT, preferred_element_type=jnp.float32)
    stats = jnp.concatenate(stats).T[:8]
    sums_ref[:32] = jnp.where(me == 0, sums[:32], sums[32:])
    send_ref[:32] = jnp.where(me == 0, sums[32:], sums[:32])
    sums_ref[32:40] = stats
    send_ref[32:40] = stats
    sums_ref[40:] = side_ref[:32]
    send_ref[40:] = side_ref[32:]


def norm(where, *arrays):
    shape = jax.ShapeDtypeStruct((72, HD), jnp.float32)
    return pl.pallas_call(
        norm_kernel,
        out_shape=(shape, shape),
        in_specs=[spec(SMEM)] + [spec(VMEM)] * 7,
        out_specs=(spec(VMEM), spec(VMEM)),
        compiler_params=pltpu.CompilerParams(vmem_limit_bytes=16 * 2**20),
        name="norm",
    )(where, *arrays)


def finish_kernel(where_ref, time_ref, own_ref, came_ref, noisy_ref, out_ref):
    me = where_ref[1]
    ours = (lax.broadcasted_iota(jnp.int32, (32, HD), 1) < DEV_ROWS) == (me == 0)
    tilt = jnp.where(ours, own_ref[40:, 0:1], came_ref[40:, 0:1])
    offset = jnp.where(ours, own_ref[40:, 1:2], came_ref[40:, 1:2])
    gap = 0.5 * (own_ref[32:33] - came_ref[32:33])
    gap = jnp.where(me == 0, gap, -gap)
    var = (own_ref[33:34] + came_ref[33:34]) / WIDTH + gap * gap
    prediction = (own_ref[:32] + came_ref[:32] + gap * tilt) / jnp.sqrt(var + EPS) + offset
    conditional, unconditional = prediction[:, :DEV_ROWS], pltpu.roll(prediction, DEV_ROWS, 1)[:, :DEV_ROWS]
    guided = unconditional + GUIDE * (conditional - unconditional)
    progress = 1.0 - time_ref[0].astype(jnp.float32) / STEPS
    sigma = SHIFT * progress / (1.0 + (SHIFT - 1.0) * progress)
    out_ref[...] = noisy_ref[...] - sigma * guided


def finish(where, timestep, own, came, noisy):
    return pl.pallas_call(
        finish_kernel,
        out_shape=jax.ShapeDtypeStruct((32, DEV_ROWS), jnp.float32),
        in_specs=[spec(SMEM)] * 2 + [spec(VMEM)] * 3,
        out_specs=spec(VMEM),
        compiler_params=pltpu.CompilerParams(vmem_limit_bytes=16 * 2**20),
        name="finish",
    )(where, timestep, own, came, noisy)


SWAP = [(0, 1), (1, 0)]
EVEN = [(i, i ^ 1) for i in range(8)]
ODD = [(i, ((i ^ 1) + (2 if i % 2 else -2)) % 8) for i in range(8)]
CORES = [EVEN + [(8 + i, 8 + j) for i, j in ODD], ODD + [(8 + i, 8 + j) for i, j in EVEN]]


def spread_pairs():
    pairs = []
    for c in range(2):
        for k in range(2):
            for l in range(2):
                pairs.append(((c * 2 + k) * 2 + l, (k * 2 + l) * 2 + c))
    return pairs


def tie(*arrays):
    return lax.optimization_barrier(arrays)


def shards(qkv, residual, out_weight, final_weight, modulation, frames, timestep, noisy):
    branch = lax.axis_index("c")
    where = jnp.stack([lax.axis_index("k"), branch, lax.axis_index("z")]).astype(jnp.int32)
    fw = final_weight.T

    block = lax.ppermute(out_weight.T, ("c", "k", "l"), spread_pairs())
    packed, block = tie(pack(qkv[0, :, 0]), block)
    unit = lax.all_to_all(jnp.broadcast_to(block, (8, 192, HD)), "y", 0, 0, tiled=True).reshape(HALF, HD)
    gathered = lax.all_to_all(packed, ("y", "k"), 0, 0, tiled=True)

    residual_rows, _ = tie(residual[0, 0], block)
    own, there, mod_half, fw_half, sides = prepare(where, residual_rows, modulation[0], fw)
    unit, there = tie(unit, there)

    units = [jnp.stack([unit, lax.ppermute(unit, ("k", "z"), CORES[0])])]
    there, _ = tie(there, units[0])
    other = lax.ppermute(there, "c", SWAP)
    units.append(lax.ppermute(units[0], ("k", "z"), CORES[1]))
    units[1], other = tie(units[1], other)
    for step in (0, 1):
        units.append(lax.ppermute(units[-1], ("k", "z"), CORES[step]))

    gathered, _ = tie(gathered, units[0])
    heads = attend(frames[0], gathered)
    rows = lax.all_to_all(heads.reshape(16, 128, HD), ("c", "y"), 0, 0, tiled=True).reshape(2, 8, 128, HD)

    keep, send = project(where, rows, units)
    came = lax.ppermute(send, "k", SWAP)
    sums, partner_sums = norm(where, keep, came, own, other, mod_half, fw_half, sides)
    came_sums = lax.ppermute(partner_sums, "c", SWAP)
    return finish(where, timestep, sums, came_sums, noisy[0].T).T[None]


def solution(mesh):
    fine = Mesh(mesh.devices.reshape(2, 8, 2, 2, 8), ("c", "y", "k", "l", "z"))
    seq, req = ("y", "k"), ("l", "z")
    return jax.shard_map(
        shards,
        mesh=fine,
        in_specs=(
            P("c", None, req, seq, None),
            P("c", req, seq, None),
            P(req, seq),
            P(),
            P("c", None, None),
            P(req, None),
            P(),
            P(req, seq, "c"),
        ),
        out_specs=P(req, seq, "c"),
        check_vma=False,
    )
```

```python
import functools

import jax
import jax.numpy as jnp
import numpy as np
from jax import lax
from jax.experimental import pallas as pl
from jax.experimental.pallas import tpu as pltpu
from jax.sharding import Mesh, PartitionSpec as P

HD = 128
STEPS = 50
FRAME_TOK = 2
GUIDE = 6.0
SHIFT = 7.0
EPS = 1e-06
FILL = -1e30
ROWS = 1024
DEV_ROWS = 64
HALF = 1536
WIDTH = 3072
LOG2E = 1.4426950408889634

NT = (((1,), (1,)), ((), ()))
VMEM = pltpu.VMEM
SMEM = pltpu.SMEM


def spec(space):
    return pl.BlockSpec(memory_space=space)


def pack_kernel(where_ref, in_ref, out_ref):
    l = where_ref[4]
    for y in range(8):
        for k in range(2):
            first = pl.multiple_of((8 * lax.bitwise_xor(l, k) + y) * HD, HD)
            out_ref[2 * y + k] = in_ref[:, :, pl.ds(first, HD)]


def pack(where, own):
    return pl.pallas_call(
        pack_kernel,
        out_shape=jax.ShapeDtypeStruct((16, 3, DEV_ROWS, HD), jnp.bfloat16),
        in_specs=[spec(SMEM), spec(VMEM)],
        out_specs=spec(VMEM),
        name="pack",
    )(where, own)


BLOCKS = ((0, 128, 0, 256), (128, 256, 0, 1024), (256, 512, 128, 1024), (512, 768, 128, 1024), (768, 1024, 128, 1024))


def attend_kernel(frames_ref, x_ref, out_ref):
    ends = []
    total = jnp.int32(0)
    for r in range(8):
        total = total + ((frames_ref[r] - 1) // 4 + 1) * FRAME_TOK
        ends.append(total)

    def ids(shape, dim, first):
        place = lax.broadcasted_iota(jnp.int32, shape, dim) + first
        found = jnp.zeros(shape, jnp.int32)
        for end in ends:
            found = found + (place >= end).astype(jnp.int32)
        return found

    scale = HD**-0.5 * LOG2E
    for first, last, low, high in BLOCKS:
        n, m = last - first, high - low
        q = x_ref[first // 64 : last // 64, 0].reshape(n, HD)
        k = x_ref[low // 64 : high // 64, 1].reshape(m, HD)
        v = x_ref[low // 64 : high // 64, 2].reshape(m, HD)
        scores = lax.dot_general(q, k, NT, preferred_element_type=jnp.float32)
        same = ids((n, 1), 0, first) == ids((1, m), 1, low)
        scores = jnp.where(same, scores, FILL)
        largest = jnp.max(scores, axis=1, keepdims=True)
        weights = jnp.exp2((scores - largest) * scale)
        denominator = jnp.sum(weights, axis=1, keepdims=True)
        mixed = jnp.dot(weights.astype(jnp.bfloat16), v, preferred_element_type=jnp.float32)
        result = (mixed / denominator).astype(jnp.bfloat16).reshape(n // 128, 128, HD)
        out_ref[0, first // 128 : last // 128] = result
        out_ref[1, first // 128 : last // 128] = result


def attend(frames, gathered):
    return pl.pallas_call(
        attend_kernel,
        out_shape=jax.ShapeDtypeStruct((2, 8, 128, HD), jnp.bfloat16),
        in_specs=[spec(SMEM), spec(VMEM)],
        out_specs=spec(VMEM),
        compiler_params=pltpu.CompilerParams(vmem_limit_bytes=32 * 2**20),
        cost_estimate=pl.CostEstimate(flops=540_000_000, bytes_accessed=2_000_000, transcendentals=1_000_000),
        name="attend",
    )(frames, gathered)


def project_kernel(where_ref, x_ref, *refs):
    units, (keep_ref, send_ref, buffer, arrived) = refs[:4], refs[4:]
    copy = pltpu.make_async_copy(units[3], buffer, arrived)
    copy.start()
    buffers = [*units[:3], buffer]
    core, z = where_ref[0], where_ref[2]
    sign = (2 * lax.rem(z, 2) - 1) * (1 - 2 * core)
    heads = [lax.rem(z + offset * sign + 8, 8) for offset in (0, -1, 1, 2, -2, -3, 3, 4)]
    x = jnp.concatenate([x_ref[:, h].reshape(256, HD) for h in heads], axis=1)
    copy.wait()
    tile = 384
    for t in range(HALF // tile):
        cols = slice(t * tile, (t + 1) * tile)
        w = jnp.concatenate([buffers[i // 2][i % 2, cols] for i in range(8)], axis=1)
        part = lax.dot_general(x, w, NT, preferred_element_type=jnp.float32)
        for b in range(2):
            low = part[b * 128 : b * 128 + 64]
            high = part[b * 128 + 64 : b * 128 + 128]
            keep_ref[b, :, cols] = jnp.where(core == 0, low, high)
            send_ref[b, :, cols] = jnp.where(core == 0, high, low).astype(jnp.bfloat16)


def project(where, x, units):
    return pl.pallas_call(
        project_kernel,
        out_shape=(
            jax.ShapeDtypeStruct((2, DEV_ROWS, HALF), jnp.float32),
            jax.ShapeDtypeStruct((2, DEV_ROWS, HALF), jnp.bfloat16),
        ),
        in_specs=[spec(SMEM)] + [spec(VMEM)] * 4 + [spec(pl.ANY)],
        out_specs=(spec(VMEM), spec(VMEM)),
        scratch_shapes=[VMEM((2, HALF, HD), jnp.bfloat16), pltpu.SemaphoreType.DMA],
        compiler_params=pltpu.CompilerParams(vmem_limit_bytes=24 * 2**20),
        cost_estimate=pl.CostEstimate(flops=810_000_000, bytes_accessed=5_000_000, transcendentals=0),
        name="project",
    )(where, x, *units)


def split3(x):
    terms = []
    for _ in range(3):
        terms.append(x.astype(jnp.bfloat16))
        x = x - terms[-1].astype(jnp.float32)
    return terms


def blocks_of(array, half):
    even, odd = [
        jnp.concatenate([array[:, (2 * i + k) * 192 : (2 * i + k + 1) * 192] for i in range(8)], axis=1) for k in range(2)
    ]
    return jnp.where(half == 0, even, odd)


def prepare_kernel(where_ref, residual_ref, mod_ref, fw_ref, own_ref, there_ref, mod_half_ref, fw_half_ref, side_ref):
    me, half = where_ref[1], where_ref[3]
    residual = residual_ref[...].astype(jnp.float32)
    own_ref[...] = blocks_of(residual, half).astype(jnp.bfloat16)
    mod_half_ref[...] = blocks_of(mod_ref[...], half)
    fw_half_ref[...] = blocks_of(fw_ref[...].astype(jnp.float32), half).astype(jnp.bfloat16)
    there_ref[:DEV_ROWS] = blocks_of(residual, 1 - half).astype(jnp.bfloat16)
    terms = split3(blocks_of(mod_ref[...], 1 - half))
    terms.append(jnp.zeros((7, HALF), jnp.bfloat16))
    there_ref[DEV_ROWS:] = jnp.concatenate([term.astype(jnp.float32) for term in terms]).astype(jnp.bfloat16)
    fw = fw_ref[...].astype(jnp.float32)
    sign = jnp.where(lax.rem(lax.broadcasted_iota(jnp.int32, (1, WIDTH), 1) // 192, 2) == 0, 1.0, -1.0)
    tilt = jnp.sum(fw * ((1.0 + mod_ref[2:3]) * sign), axis=1, keepdims=True)
    offset = jnp.sum(fw * mod_ref[1:2], axis=1, keepdims=True)
    lane = lax.broadcasted_iota(jnp.int32, (64, HD), 1)
    side = jnp.where(lane == 0, tilt, jnp.where(lane == 1, offset, 0.0))
    side_ref[:32] = jnp.where(me == 0, side[:32], side[32:])
    side_ref[32:] = jnp.where(me == 0, side[32:], side[:32])


def prepare(where, residual, mod, fw):
    return pl.pallas_call(
        prepare_kernel,
        out_shape=(
            jax.ShapeDtypeStruct((DEV_ROWS, HALF), jnp.bfloat16),
            jax.ShapeDtypeStruct((DEV_ROWS + 16, HALF), jnp.bfloat16),
            jax.ShapeDtypeStruct((3, HALF), jnp.float32),
            jax.ShapeDtypeStruct((64, HALF), jnp.bfloat16),
            jax.ShapeDtypeStruct((64, HD), jnp.float32),
        ),
        in_specs=[spec(SMEM)] + [spec(VMEM)] * 3,
        out_specs=(spec(VMEM),) * 5,
        compiler_params=pltpu.CompilerParams(vmem_limit_bytes=16 * 2**20),
        name="prepare",
    )(where, residual, mod, fw)


def norm_kernel(where_ref, keep_ref, came_ref, own_ref, other_ref, mod_ref, fw_ref, side_ref, sums_ref, send_ref):
    me = where_ref[1]
    own = own_ref[...].astype(jnp.float32)
    other = other_ref[:DEV_ROWS].astype(jnp.float32)
    tail = other_ref[DEV_ROWS:].astype(jnp.float32)
    mod_own, mod_other = mod_ref[...], tail[0:3] + tail[3:6] + tail[6:9]
    lane = lax.broadcasted_iota(jnp.int32, (DEV_ROWS, HD), 1)
    scaled, stats = [], []
    for b in range(2):
        mod = jnp.where(me == b, mod_own, mod_other)
        attn_out = (keep_ref[b] + came_ref[b].astype(jnp.float32)).astype(jnp.bfloat16).astype(jnp.float32)
        stream = jnp.where(me == b, own, other) + mod[0:1] * attn_out
        mean = jnp.mean(stream, axis=1, keepdims=True)
        centered = stream - mean
        spread = jnp.sum(centered * centered, axis=1, keepdims=True)
        scaled.append((centered * (1.0 + mod[2:3])).astype(jnp.bfloat16))
        stats.append(jnp.where(lane == 0, mean, jnp.where(lane == 1, spread, 0.0)))
    sums = lax.dot_general(fw_ref[...], jnp.concatenate(scaled), NT, preferred_element_type=jnp.float32)
    stats = jnp.concatenate(stats).T[:8]
    sums_ref[:32] = jnp.where(me == 0, sums[:32], sums[32:])
    send_ref[:32] = jnp.where(me == 0, sums[32:], sums[:32])
    sums_ref[32:40] = stats
    send_ref[32:40] = stats
    sums_ref[40:] = side_ref[:32]
    send_ref[40:] = side_ref[32:]


def norm(where, *arrays):
    shape = jax.ShapeDtypeStruct((72, HD), jnp.float32)
    return pl.pallas_call(
        norm_kernel,
        out_shape=(shape, shape),
        in_specs=[spec(SMEM)] + [spec(VMEM)] * 7,
        out_specs=(spec(VMEM), spec(VMEM)),
        compiler_params=pltpu.CompilerParams(vmem_limit_bytes=16 * 2**20),
        name="norm",
    )(where, *arrays)


def finish_kernel(where_ref, time_ref, own_ref, came_ref, noisy_ref, out_ref):
    me = where_ref[1]
    ours = (lax.broadcasted_iota(jnp.int32, (32, HD), 1) < DEV_ROWS) == (me == 0)
    tilt = jnp.where(ours, own_ref[40:, 0:1], came_ref[40:, 0:1])
    offset = jnp.where(ours, own_ref[40:, 1:2], came_ref[40:, 1:2])
    gap = 0.5 * (own_ref[32:33] - came_ref[32:33])
    gap = jnp.where(where_ref[3] == 0, gap, -gap)
    var = (own_ref[33:34] + came_ref[33:34]) / WIDTH + gap * gap
    prediction = (own_ref[:32] + came_ref[:32] + gap * tilt) / jnp.sqrt(var + EPS) + offset
    conditional, unconditional = prediction[:, :DEV_ROWS], pltpu.roll(prediction, DEV_ROWS, 1)[:, :DEV_ROWS]
    guided = unconditional + GUIDE * (conditional - unconditional)
    progress = 1.0 - time_ref[0].astype(jnp.float32) / STEPS
    sigma = SHIFT * progress / (1.0 + (SHIFT - 1.0) * progress)
    out_ref[...] = noisy_ref[...] - sigma * guided


def finish(where, timestep, own, came, noisy):
    return pl.pallas_call(
        finish_kernel,
        out_shape=jax.ShapeDtypeStruct((32, DEV_ROWS), jnp.float32),
        in_specs=[spec(SMEM)] * 2 + [spec(VMEM)] * 3,
        out_specs=spec(VMEM),
        compiler_params=pltpu.CompilerParams(vmem_limit_bytes=16 * 2**20),
        name="finish",
    )(where, timestep, own, came, noisy)


SWAP = [(0, 1), (1, 0)]
EVEN = [(i, i ^ 1) for i in range(8)]
ODD = [(i, ((i ^ 1) + (2 if i % 2 else -2)) % 8) for i in range(8)]
CORES = [EVEN + [(8 + i, 8 + j) for i, j in ODD], ODD + [(8 + i, 8 + j) for i, j in EVEN]]


def spread_pairs():
    pairs = []
    for c in range(2):
        for k in range(2):
            for l in range(2):
                chip = c ^ k
                pairs.append(((c * 2 + k) * 2 + l, (c * 2 + (chip ^ l)) * 2 + chip))
    return pairs


def tie(*arrays):
    return lax.optimization_barrier(arrays)


def shards(qkv, residual, out_weight, final_weight, modulation, frames, timestep, noisy):
    branch = lax.axis_index("c")
    l = lax.axis_index("l")
    where = jnp.stack([lax.axis_index("k"), branch, lax.axis_index("z"), lax.bitwise_xor(branch, l), l]).astype(jnp.int32)
    fw = final_weight.T

    block = lax.ppermute(out_weight.T, ("c", "k", "l"), spread_pairs())
    unit = lax.all_to_all(jnp.broadcast_to(block, (8, 192, HD)), "y", 0, 0, tiled=True).reshape(HALF, HD)

    qkv_rows, residual_rows, _ = tie(qkv[0, :, 0], residual[0, 0], block)
    packed = pack(where, qkv_rows)
    own, there, mod_half, fw_half, sides = prepare(where, residual_rows, modulation[0], fw)
    unit, there, packed = tie(unit, there, packed)
    gathered = lax.all_to_all(packed, ("y", "k"), 0, 0, tiled=True)

    units = [jnp.stack([unit, lax.ppermute(unit, ("k", "z"), CORES[0])])]
    there, _ = tie(there, units[0])
    other = lax.ppermute(there, "c", SWAP)
    units.append(lax.ppermute(units[0], ("k", "z"), CORES[1]))
    units[1], other = tie(units[1], other)
    for step in (0, 1):
        units.append(lax.ppermute(units[-1], ("k", "z"), CORES[step]))

    heads = attend(frames[0], gathered)
    rows = lax.all_to_all(heads.reshape(16, 128, HD), ("c", "y"), 0, 0, tiled=True).reshape(2, 8, 128, HD)

    keep, send = project(where, rows, units)
    came = lax.ppermute(send, "k", SWAP)
    sums, partner_sums = norm(where, keep, came, own, other, mod_half, fw_half, sides)
    came_sums = lax.ppermute(partner_sums, "c", SWAP)
    return finish(where, timestep, sums, came_sums, noisy[0].T).T[None]


def solution(mesh):
    fine = Mesh(mesh.devices.reshape(2, 8, 2, 2, 8), ("c", "y", "k", "l", "z"))
    seq, req = ("y", "k"), ("l", "z")
    return jax.shard_map(
        shards,
        mesh=fine,
        in_specs=(
            P("c", None, req, seq, None),
            P("c", req, seq, None),
            P(req, seq),
            P(),
            P("c", None, None),
            P(req, None),
            P(),
            P(req, seq, "c"),
        ),
        out_specs=P(req, seq, "c"),
        check_vma=False,
    )
```

```python
import functools

import jax
import jax.numpy as jnp
import numpy as np
from jax import lax
from jax.experimental import pallas as pl
from jax.experimental.pallas import tpu as pltpu
from jax.sharding import Mesh, PartitionSpec as P

HD = 128
STEPS = 50
FRAME_TOK = 2
GUIDE = 6.0
SHIFT = 7.0
EPS = 1e-06
FILL = -1e30
ROWS = 1024
DEV_ROWS = 64
HALF = 1536
WIDTH = 3072
LOG2E = 1.4426950408889634

NT = (((1,), (1,)), ((), ()))
VMEM = pltpu.VMEM
SMEM = pltpu.SMEM


def spec(space):
    return pl.BlockSpec(memory_space=space)


def pack_kernel(where_ref, in_ref, out_ref):
    l = where_ref[4]
    for y in range(8):
        for k in range(2):
            first = pl.multiple_of((8 * lax.bitwise_xor(l, k) + y) * HD, HD)
            out_ref[2 * y + k] = in_ref[:, :, pl.ds(first, HD)]


def pack(where, own):
    return pl.pallas_call(
        pack_kernel,
        out_shape=jax.ShapeDtypeStruct((16, 3, DEV_ROWS, HD), jnp.bfloat16),
        in_specs=[spec(SMEM), spec(VMEM)],
        out_specs=spec(VMEM),
        name="pack",
    )(where, own)


BLOCKS = ((0, 128, 0, 256), (128, 256, 0, 1024), (256, 512, 128, 1024), (512, 768, 128, 1024), (768, 1024, 128, 1024))


def attend_kernel(frames_ref, x_ref, out_ref):
    ends = []
    total = jnp.int32(0)
    for r in range(8):
        total = total + ((frames_ref[r] - 1) // 4 + 1) * FRAME_TOK
        ends.append(total)

    def ids(shape, dim, first):
        place = lax.broadcasted_iota(jnp.int32, shape, dim) + first
        found = jnp.zeros(shape, jnp.int32)
        for end in ends:
            found = found + (place >= end).astype(jnp.int32)
        return found

    scale = HD**-0.5 * LOG2E
    for first, last, low, high in BLOCKS:
        n, m = last - first, high - low
        q = x_ref[first // 64 : last // 64, 0].reshape(n, HD)
        k = x_ref[low // 64 : high // 64, 1].reshape(m, HD)
        v = x_ref[low // 64 : high // 64, 2].reshape(m, HD)
        scores = lax.dot_general(q, k, NT, preferred_element_type=jnp.float32)
        same = ids((n, 1), 0, first) == ids((1, m), 1, low)
        scores = jnp.where(same, scores, FILL)
        largest = jnp.max(scores, axis=1, keepdims=True)
        weights = jnp.exp2((scores - largest) * scale)
        denominator = jnp.sum(weights, axis=1, keepdims=True)
        mixed = jnp.dot(weights.astype(jnp.bfloat16), v, preferred_element_type=jnp.float32)
        result = (mixed / denominator).astype(jnp.bfloat16).reshape(n // 128, 128, HD)
        out_ref[first // 128 : last // 128] = result


def attend(frames, gathered):
    return pl.pallas_call(
        attend_kernel,
        out_shape=jax.ShapeDtypeStruct((8, 128, HD), jnp.bfloat16),
        in_specs=[spec(SMEM), spec(VMEM)],
        out_specs=spec(VMEM),
        compiler_params=pltpu.CompilerParams(vmem_limit_bytes=32 * 2**20),
        cost_estimate=pl.CostEstimate(flops=540_000_000, bytes_accessed=2_000_000, transcendentals=1_000_000),
        name="attend",
    )(frames, gathered)


def project_kernel(where_ref, x_ref, *refs):
    units, (keep_ref, send_ref, buffer, arrived) = refs[:4], refs[4:]
    copy = pltpu.make_async_copy(units[3], buffer, arrived)
    copy.start()
    buffers = [*units[:3], buffer]
    core, z = where_ref[0], where_ref[2]
    sign = (2 * lax.rem(z, 2) - 1) * (1 - 2 * core)
    heads = [lax.rem(z + offset * sign + 8, 8) for offset in (0, -1, 1, 2, -2, -3, 3, 4)]
    x = jnp.concatenate([x_ref[:, h].reshape(256, HD) for h in heads], axis=1)
    copy.wait()
    tile = 384
    for t in range(HALF // tile):
        cols = slice(t * tile, (t + 1) * tile)
        w = jnp.concatenate([buffers[i // 2][i % 2, cols] for i in range(8)], axis=1)
        part = lax.dot_general(x, w, NT, preferred_element_type=jnp.float32)
        for b in range(2):
            low = part[b * 128 : b * 128 + 64]
            high = part[b * 128 + 64 : b * 128 + 128]
            keep_ref[b, :, cols] = jnp.where(core == 0, low, high)
            send_ref[b, :, cols] = jnp.where(core == 0, high, low).astype(jnp.bfloat16)


def project(where, x, units):
    return pl.pallas_call(
        project_kernel,
        out_shape=(
            jax.ShapeDtypeStruct((2, DEV_ROWS, HALF), jnp.float32),
            jax.ShapeDtypeStruct((2, DEV_ROWS, HALF), jnp.bfloat16),
        ),
        in_specs=[spec(SMEM)] + [spec(VMEM)] * 4 + [spec(pl.ANY)],
        out_specs=(spec(VMEM), spec(VMEM)),
        scratch_shapes=[VMEM((2, HALF, HD), jnp.bfloat16), pltpu.SemaphoreType.DMA],
        compiler_params=pltpu.CompilerParams(vmem_limit_bytes=24 * 2**20),
        cost_estimate=pl.CostEstimate(flops=810_000_000, bytes_accessed=5_000_000, transcendentals=0),
        name="project",
    )(where, x, *units)


def split3(x):
    terms = []
    for _ in range(3):
        terms.append(x.astype(jnp.bfloat16))
        x = x - terms[-1].astype(jnp.float32)
    return terms


def blocks_of(array, half):
    even, odd = [
        jnp.concatenate([array[:, (2 * i + k) * 192 : (2 * i + k + 1) * 192] for i in range(8)], axis=1) for k in range(2)
    ]
    return jnp.where(half == 0, even, odd)


def prepare_kernel(where_ref, residual_ref, mod_ref, fw_ref, own_ref, there_ref, mod_half_ref, fw_half_ref, side_ref):
    me, half = where_ref[1], where_ref[3]
    residual = residual_ref[...].astype(jnp.float32)
    own_ref[...] = blocks_of(residual, half).astype(jnp.bfloat16)
    mod_half_ref[...] = blocks_of(mod_ref[...], half)
    fw_half_ref[...] = blocks_of(fw_ref[...].astype(jnp.float32), half).astype(jnp.bfloat16)
    there_ref[:DEV_ROWS] = blocks_of(residual, 1 - half).astype(jnp.bfloat16)
    terms = split3(blocks_of(mod_ref[...], 1 - half))
    terms.append(jnp.zeros((7, HALF), jnp.bfloat16))
    there_ref[DEV_ROWS:] = jnp.concatenate([term.astype(jnp.float32) for term in terms]).astype(jnp.bfloat16)
    fw = fw_ref[...].astype(jnp.float32)
    sign = jnp.where(lax.rem(lax.broadcasted_iota(jnp.int32, (1, WIDTH), 1) // 192, 2) == 0, 1.0, -1.0)
    tilt = jnp.sum(fw * ((1.0 + mod_ref[2:3]) * sign), axis=1, keepdims=True)
    offset = jnp.sum(fw * mod_ref[1:2], axis=1, keepdims=True)
    lane = lax.broadcasted_iota(jnp.int32, (64, HD), 1)
    side = jnp.where(lane == 0, tilt, jnp.where(lane == 1, offset, 0.0))
    side_ref[:32] = jnp.where(me == 0, side[:32], side[32:])
    side_ref[32:] = jnp.where(me == 0, side[32:], side[:32])


def prepare(where, residual, mod, fw):
    return pl.pallas_call(
        prepare_kernel,
        out_shape=(
            jax.ShapeDtypeStruct((DEV_ROWS, HALF), jnp.bfloat16),
            jax.ShapeDtypeStruct((DEV_ROWS + 16, HALF), jnp.bfloat16),
            jax.ShapeDtypeStruct((3, HALF), jnp.float32),
            jax.ShapeDtypeStruct((64, HALF), jnp.bfloat16),
            jax.ShapeDtypeStruct((64, HD), jnp.float32),
        ),
        in_specs=[spec(SMEM)] + [spec(VMEM)] * 3,
        out_specs=(spec(VMEM),) * 5,
        compiler_params=pltpu.CompilerParams(vmem_limit_bytes=16 * 2**20),
        name="prepare",
    )(where, residual, mod, fw)


def norm_kernel(where_ref, keep_ref, came_ref, own_ref, other_ref, mod_ref, fw_ref, side_ref, sums_ref, send_ref):
    me = where_ref[1]
    own = own_ref[...].astype(jnp.float32)
    other = other_ref[:DEV_ROWS].astype(jnp.float32)
    tail = other_ref[DEV_ROWS:].astype(jnp.float32)
    mod_own, mod_other = mod_ref[...], tail[0:3] + tail[3:6] + tail[6:9]
    lane = lax.broadcasted_iota(jnp.int32, (DEV_ROWS, HD), 1)
    scaled, stats = [], []
    for b in range(2):
        mod = jnp.where(me == b, mod_own, mod_other)
        attn_out = (keep_ref[b] + came_ref[b].astype(jnp.float32)).astype(jnp.bfloat16).astype(jnp.float32)
        stream = jnp.where(me == b, own, other) + mod[0:1] * attn_out
        mean = jnp.mean(stream, axis=1, keepdims=True)
        centered = stream - mean
        spread = jnp.sum(centered * centered, axis=1, keepdims=True)
        scaled.append((centered * (1.0 + mod[2:3])).astype(jnp.bfloat16))
        stats.append(jnp.where(lane == 0, mean, jnp.where(lane == 1, spread, 0.0)))
    sums = lax.dot_general(fw_ref[...], jnp.concatenate(scaled), NT, preferred_element_type=jnp.float32)
    stats = jnp.concatenate(stats).T[:8]
    sums_ref[:32] = jnp.where(me == 0, sums[:32], sums[32:])
    send_ref[:32] = jnp.where(me == 0, sums[32:], sums[:32])
    sums_ref[32:40] = stats
    send_ref[32:40] = stats
    sums_ref[40:] = side_ref[:32]
    send_ref[40:] = side_ref[32:]


def norm(where, *arrays):
    shape = jax.ShapeDtypeStruct((72, HD), jnp.float32)
    return pl.pallas_call(
        norm_kernel,
        out_shape=(shape, shape),
        in_specs=[spec(SMEM)] + [spec(VMEM)] * 7,
        out_specs=(spec(VMEM), spec(VMEM)),
        compiler_params=pltpu.CompilerParams(vmem_limit_bytes=16 * 2**20),
        name="norm",
    )(where, *arrays)


def finish_kernel(where_ref, time_ref, own_ref, came_ref, noisy_ref, out_ref):
    me = where_ref[1]
    ours = (lax.broadcasted_iota(jnp.int32, (32, HD), 1) < DEV_ROWS) == (me == 0)
    tilt = jnp.where(ours, own_ref[40:, 0:1], came_ref[40:, 0:1])
    offset = jnp.where(ours, own_ref[40:, 1:2], came_ref[40:, 1:2])
    gap = 0.5 * (own_ref[32:33] - came_ref[32:33])
    gap = jnp.where(where_ref[3] == 0, gap, -gap)
    var = (own_ref[33:34] + came_ref[33:34]) / WIDTH + gap * gap
    prediction = (own_ref[:32] + came_ref[:32] + gap * tilt) / jnp.sqrt(var + EPS) + offset
    conditional, unconditional = prediction[:, :DEV_ROWS], pltpu.roll(prediction, DEV_ROWS, 1)[:, :DEV_ROWS]
    guided = unconditional + GUIDE * (conditional - unconditional)
    progress = 1.0 - time_ref[0].astype(jnp.float32) / STEPS
    sigma = SHIFT * progress / (1.0 + (SHIFT - 1.0) * progress)
    out_ref[...] = noisy_ref[...] - sigma * guided


def finish(where, timestep, own, came, noisy):
    return pl.pallas_call(
        finish_kernel,
        out_shape=jax.ShapeDtypeStruct((32, DEV_ROWS), jnp.float32),
        in_specs=[spec(SMEM)] * 2 + [spec(VMEM)] * 3,
        out_specs=spec(VMEM),
        compiler_params=pltpu.CompilerParams(vmem_limit_bytes=16 * 2**20),
        name="finish",
    )(where, timestep, own, came, noisy)


SWAP = [(0, 1), (1, 0)]
EVEN = [(i, i ^ 1) for i in range(8)]
ODD = [(i, ((i ^ 1) + (2 if i % 2 else -2)) % 8) for i in range(8)]
CORES = [EVEN + [(8 + i, 8 + j) for i, j in ODD], ODD + [(8 + i, 8 + j) for i, j in EVEN]]


def spread_pairs():
    pairs = []
    for c in range(2):
        for k in range(2):
            for l in range(2):
                chip = c ^ k
                pairs.append(((c * 2 + k) * 2 + l, (c * 2 + (chip ^ l)) * 2 + chip))
    return pairs


def tie(*arrays):
    return lax.optimization_barrier(arrays)


def shards(qkv, residual, out_weight, final_weight, modulation, frames, timestep, noisy):
    branch = lax.axis_index("c")
    l = lax.axis_index("l")
    where = jnp.stack([lax.axis_index("k"), branch, lax.axis_index("z"), lax.bitwise_xor(branch, l), l]).astype(jnp.int32)
    fw = final_weight.T

    block = lax.ppermute(out_weight.T, ("c", "k", "l"), spread_pairs())
    unit = lax.all_to_all(jnp.broadcast_to(block, (8, 192, HD)), "y", 0, 0, tiled=True).reshape(HALF, HD)

    qkv_rows, residual_rows, _ = tie(qkv[0, :, 0], residual[0, 0], block)
    packed = pack(where, qkv_rows)
    own, there, mod_half, fw_half, sides = prepare(where, residual_rows, modulation[0], fw)
    unit, there, packed = tie(unit, there, packed)
    gathered = lax.all_to_all(packed, ("y", "k"), 0, 0, tiled=True)

    units = [jnp.stack([unit, lax.ppermute(unit, ("k", "z"), CORES[0])])]
    there, _ = tie(there, units[0])
    other = lax.ppermute(there, "c", SWAP)
    units.append(lax.ppermute(units[0], ("k", "z"), CORES[1]))
    units[1], other = tie(units[1], other)
    for step in (0, 1):
        units.append(lax.ppermute(units[-1], ("k", "z"), CORES[step]))

    heads = attend(frames[0], gathered)
    heads = jnp.broadcast_to(heads, (2, 8, 128, HD)).reshape(16, 128, HD)
    rows = lax.all_to_all(heads, ("c", "y"), 0, 0, tiled=True).reshape(2, 8, 128, HD)

    keep, send = project(where, rows, units)
    came = lax.ppermute(send, "k", SWAP)
    sums, partner_sums = norm(where, keep, came, own, other, mod_half, fw_half, sides)
    came_sums = lax.ppermute(partner_sums, "c", SWAP)
    return finish(where, timestep, sums, came_sums, noisy[0].T).T[None]


def solution(mesh):
    fine = Mesh(mesh.devices.reshape(2, 8, 2, 2, 8), ("c", "y", "k", "l", "z"))
    seq, req = ("y", "k"), ("l", "z")
    return jax.shard_map(
        shards,
        mesh=fine,
        in_specs=(
            P("c", None, req, seq, None),
            P("c", req, seq, None),
            P(req, seq),
            P(),
            P("c", None, None),
            P(req, None),
            P(),
            P(req, seq, "c"),
        ),
        out_specs=P(req, seq, "c"),
        check_vma=False,
    )
```

```python
import functools

import jax
import jax.numpy as jnp
import numpy as np
from jax import lax
from jax.experimental import pallas as pl
from jax.experimental.pallas import tpu as pltpu
from jax.sharding import Mesh, PartitionSpec as P

HD = 128
STEPS = 50
FRAME_TOK = 2
GUIDE = 6.0
SHIFT = 7.0
EPS = 1e-06
FILL = -1e30
ROWS = 1024
DEV_ROWS = 64
HALF = 1536
WIDTH = 3072
LOG2E = 1.4426950408889634

NT = (((1,), (1,)), ((), ()))
VMEM = pltpu.VMEM
SMEM = pltpu.SMEM


def spec(space):
    return pl.BlockSpec(memory_space=space)


def pack_kernel(where_ref, in_ref, out_ref):
    l = where_ref[4]
    for y in range(8):
        for k in range(2):
            first = pl.multiple_of((8 * lax.bitwise_xor(l, k) + y) * HD, HD)
            out_ref[2 * y + k] = in_ref[:, :, pl.ds(first, HD)]


def pack(where, own):
    return pl.pallas_call(
        pack_kernel,
        out_shape=jax.ShapeDtypeStruct((16, 3, DEV_ROWS, HD), jnp.bfloat16),
        in_specs=[spec(SMEM), spec(VMEM)],
        out_specs=spec(VMEM),
        name="pack",
    )(where, own)


BLOCKS = ((0, 128, 0, 256), (128, 256, 0, 1024), (256, 512, 128, 1024), (512, 768, 128, 1024), (768, 1024, 128, 1024))


def attend_kernel(frames_ref, x_ref, out_ref):
    ends = []
    total = jnp.int32(0)
    for r in range(8):
        total = total + ((frames_ref[r] - 1) // 4 + 1) * FRAME_TOK
        ends.append(total)

    def ids(shape, dim, first):
        place = lax.broadcasted_iota(jnp.int32, shape, dim) + first
        found = jnp.zeros(shape, jnp.int32)
        for end in ends:
            found = found + (place >= end).astype(jnp.int32)
        return found

    scale = HD**-0.5 * LOG2E
    for first, last, low, high in BLOCKS:
        n, m = last - first, high - low
        q = x_ref[first // 64 : last // 64, 0].reshape(n, HD)
        k = x_ref[low // 64 : high // 64, 1].reshape(m, HD)
        v = x_ref[low // 64 : high // 64, 2].reshape(m, HD)
        scores = lax.dot_general(q, k, NT, preferred_element_type=jnp.float32)
        same = ids((n, 1), 0, first) == ids((1, m), 1, low)
        scores = jnp.where(same, scores, FILL)
        largest = jnp.max(scores, axis=1, keepdims=True)
        weights = jnp.exp2((scores - largest) * scale)
        denominator = jnp.sum(weights, axis=1, keepdims=True)
        mixed = jnp.dot(weights.astype(jnp.bfloat16), v, preferred_element_type=jnp.float32)
        result = (mixed / denominator).astype(jnp.bfloat16).reshape(n // 128, 128, HD)
        out_ref[0, first // 128 : last // 128] = result
        out_ref[1, first // 128 : last // 128] = result


def attend(frames, gathered):
    return pl.pallas_call(
        attend_kernel,
        out_shape=jax.ShapeDtypeStruct((2, 8, 128, HD), jnp.bfloat16),
        in_specs=[spec(SMEM), spec(VMEM)],
        out_specs=spec(VMEM),
        compiler_params=pltpu.CompilerParams(vmem_limit_bytes=32 * 2**20),
        cost_estimate=pl.CostEstimate(flops=540_000_000, bytes_accessed=2_000_000, transcendentals=1_000_000),
        name="attend",
    )(frames, gathered)


def project_kernel(where_ref, x_ref, *refs):
    units, (keep_ref, send_ref, buffer, arrived) = refs[:4], refs[4:]
    copy = pltpu.make_async_copy(units[3], buffer, arrived)
    copy.start()
    buffers = [*units[:3], buffer]
    core, z = where_ref[0], where_ref[2]
    sign = (2 * lax.rem(z, 2) - 1) * (1 - 2 * core)
    heads = [lax.rem(z + offset * sign + 8, 8) for offset in (0, -1, 1, 2, -2, -3, 3, 4)]
    x = jnp.concatenate([x_ref[:, h].reshape(256, HD) for h in heads], axis=1)
    tile = 384
    for t in range(HALF // tile):
        cols = slice(t * tile, (t + 1) * tile)
        w = jnp.concatenate([buffers[i // 2][i % 2, cols] for i in range(6)], axis=1)
        part = lax.dot_general(x[:, : 6 * HD], w, NT, preferred_element_type=jnp.float32)
        if t == 0:
            copy.wait()
        w = jnp.concatenate([buffer[i, cols] for i in range(2)], axis=1)
        part = part + lax.dot_general(x[:, 6 * HD :], w, NT, preferred_element_type=jnp.float32)
        for b in range(2):
            low = part[b * 128 : b * 128 + 64]
            high = part[b * 128 + 64 : b * 128 + 128]
            keep_ref[b, :, cols] = jnp.where(core == 0, low, high)
            send_ref[b, :, cols] = jnp.where(core == 0, high, low).astype(jnp.bfloat16)


def project(where, x, units):
    return pl.pallas_call(
        project_kernel,
        out_shape=(
            jax.ShapeDtypeStruct((2, DEV_ROWS, HALF), jnp.float32),
            jax.ShapeDtypeStruct((2, DEV_ROWS, HALF), jnp.bfloat16),
        ),
        in_specs=[spec(SMEM)] + [spec(VMEM)] * 4 + [spec(pl.ANY)],
        out_specs=(spec(VMEM), spec(VMEM)),
        scratch_shapes=[VMEM((2, HALF, HD), jnp.bfloat16), pltpu.SemaphoreType.DMA],
        compiler_params=pltpu.CompilerParams(vmem_limit_bytes=24 * 2**20),
        cost_estimate=pl.CostEstimate(flops=810_000_000, bytes_accessed=5_000_000, transcendentals=0),
        name="project",
    )(where, x, *units)


def split3(x):
    terms = []
    for _ in range(3):
        terms.append(x.astype(jnp.bfloat16))
        x = x - terms[-1].astype(jnp.float32)
    return terms


def blocks_of(array, half):
    even, odd = [
        jnp.concatenate([array[:, (2 * i + k) * 192 : (2 * i + k + 1) * 192] for i in range(8)], axis=1) for k in range(2)
    ]
    return jnp.where(half == 0, even, odd)


def prepare_kernel(where_ref, residual_ref, mod_ref, fw_ref, own_ref, there_ref, mod_half_ref, fw_half_ref, side_ref):
    me, half = where_ref[1], where_ref[3]
    residual = residual_ref[...].astype(jnp.float32)
    own_ref[...] = blocks_of(residual, half).astype(jnp.bfloat16)
    mod_half_ref[...] = blocks_of(mod_ref[...], half)
    fw_half_ref[...] = blocks_of(fw_ref[...].astype(jnp.float32), half).astype(jnp.bfloat16)
    there_ref[:DEV_ROWS] = blocks_of(residual, 1 - half).astype(jnp.bfloat16)
    terms = split3(blocks_of(mod_ref[...], 1 - half))
    terms.append(jnp.zeros((7, HALF), jnp.bfloat16))
    there_ref[DEV_ROWS:] = jnp.concatenate([term.astype(jnp.float32) for term in terms]).astype(jnp.bfloat16)
    fw = fw_ref[...].astype(jnp.float32)
    sign = jnp.where(lax.rem(lax.broadcasted_iota(jnp.int32, (1, WIDTH), 1) // 192, 2) == 0, 1.0, -1.0)
    tilt = jnp.sum(fw * ((1.0 + mod_ref[2:3]) * sign), axis=1, keepdims=True)
    offset = jnp.sum(fw * mod_ref[1:2], axis=1, keepdims=True)
    lane = lax.broadcasted_iota(jnp.int32, (64, HD), 1)
    side = jnp.where(lane == 0, tilt, jnp.where(lane == 1, offset, 0.0))
    side_ref[:32] = jnp.where(me == 0, side[:32], side[32:])
    side_ref[32:] = jnp.where(me == 0, side[32:], side[:32])


def prepare(where, residual, mod, fw):
    return pl.pallas_call(
        prepare_kernel,
        out_shape=(
            jax.ShapeDtypeStruct((DEV_ROWS, HALF), jnp.bfloat16),
            jax.ShapeDtypeStruct((DEV_ROWS + 16, HALF), jnp.bfloat16),
            jax.ShapeDtypeStruct((3, HALF), jnp.float32),
            jax.ShapeDtypeStruct((64, HALF), jnp.bfloat16),
            jax.ShapeDtypeStruct((64, HD), jnp.float32),
        ),
        in_specs=[spec(SMEM)] + [spec(VMEM)] * 3,
        out_specs=(spec(VMEM),) * 5,
        compiler_params=pltpu.CompilerParams(vmem_limit_bytes=16 * 2**20),
        name="prepare",
    )(where, residual, mod, fw)


def norm_kernel(where_ref, keep_ref, came_ref, own_ref, other_ref, mod_ref, fw_ref, side_ref, sums_ref, send_ref):
    me = where_ref[1]
    own = own_ref[...].astype(jnp.float32)
    other = other_ref[:DEV_ROWS].astype(jnp.float32)
    tail = other_ref[DEV_ROWS:].astype(jnp.float32)
    mod_own, mod_other = mod_ref[...], tail[0:3] + tail[3:6] + tail[6:9]
    lane = lax.broadcasted_iota(jnp.int32, (DEV_ROWS, HD), 1)
    scaled, stats = [], []
    for b in range(2):
        mod = jnp.where(me == b, mod_own, mod_other)
        attn_out = (keep_ref[b] + came_ref[b].astype(jnp.float32)).astype(jnp.bfloat16).astype(jnp.float32)
        stream = jnp.where(me == b, own, other) + mod[0:1] * attn_out
        mean = jnp.mean(stream, axis=1, keepdims=True)
        centered = stream - mean
        spread = jnp.sum(centered * centered, axis=1, keepdims=True)
        scaled.append((centered * (1.0 + mod[2:3])).astype(jnp.bfloat16))
        stats.append(jnp.where(lane == 0, mean, jnp.where(lane == 1, spread, 0.0)))
    sums = lax.dot_general(fw_ref[...], jnp.concatenate(scaled), NT, preferred_element_type=jnp.float32)
    stats = jnp.concatenate(stats).T[:8]
    sums_ref[:32] = jnp.where(me == 0, sums[:32], sums[32:])
    send_ref[:32] = jnp.where(me == 0, sums[32:], sums[:32])
    sums_ref[32:40] = stats
    send_ref[32:40] = stats
    sums_ref[40:] = side_ref[:32]
    send_ref[40:] = side_ref[32:]


def norm(where, *arrays):
    shape = jax.ShapeDtypeStruct((72, HD), jnp.float32)
    return pl.pallas_call(
        norm_kernel,
        out_shape=(shape, shape),
        in_specs=[spec(SMEM)] + [spec(VMEM)] * 7,
        out_specs=(spec(VMEM), spec(VMEM)),
        compiler_params=pltpu.CompilerParams(vmem_limit_bytes=16 * 2**20),
        name="norm",
    )(where, *arrays)


def finish_kernel(where_ref, time_ref, own_ref, came_ref, noisy_ref, out_ref):
    me = where_ref[1]
    ours = (lax.broadcasted_iota(jnp.int32, (32, HD), 1) < DEV_ROWS) == (me == 0)
    tilt = jnp.where(ours, own_ref[40:, 0:1], came_ref[40:, 0:1])
    offset = jnp.where(ours, own_ref[40:, 1:2], came_ref[40:, 1:2])
    gap = 0.5 * (own_ref[32:33] - came_ref[32:33])
    gap = jnp.where(where_ref[3] == 0, gap, -gap)
    var = (own_ref[33:34] + came_ref[33:34]) / WIDTH + gap * gap
    prediction = (own_ref[:32] + came_ref[:32] + gap * tilt) / jnp.sqrt(var + EPS) + offset
    conditional, unconditional = prediction[:, :DEV_ROWS], pltpu.roll(prediction, DEV_ROWS, 1)[:, :DEV_ROWS]
    guided = unconditional + GUIDE * (conditional - unconditional)
    progress = 1.0 - time_ref[0].astype(jnp.float32) / STEPS
    sigma = SHIFT * progress / (1.0 + (SHIFT - 1.0) * progress)
    out_ref[...] = noisy_ref[...] - sigma * guided


def finish(where, timestep, own, came, noisy):
    return pl.pallas_call(
        finish_kernel,
        out_shape=jax.ShapeDtypeStruct((32, DEV_ROWS), jnp.float32),
        in_specs=[spec(SMEM)] * 2 + [spec(VMEM)] * 3,
        out_specs=spec(VMEM),
        compiler_params=pltpu.CompilerParams(vmem_limit_bytes=16 * 2**20),
        name="finish",
    )(where, timestep, own, came, noisy)


SWAP = [(0, 1), (1, 0)]
EVEN = [(i, i ^ 1) for i in range(8)]
ODD = [(i, ((i ^ 1) + (2 if i % 2 else -2)) % 8) for i in range(8)]
CORES = [EVEN + [(8 + i, 8 + j) for i, j in ODD], ODD + [(8 + i, 8 + j) for i, j in EVEN]]


def spread_pairs():
    pairs = []
    for c in range(2):
        for k in range(2):
            for l in range(2):
                chip = c ^ k
                pairs.append(((c * 2 + k) * 2 + l, (c * 2 + (chip ^ l)) * 2 + chip))
    return pairs


def tie(*arrays):
    return lax.optimization_barrier(arrays)


def shards(qkv, residual, out_weight, final_weight, modulation, frames, timestep, noisy):
    branch = lax.axis_index("c")
    l = lax.axis_index("l")
    where = jnp.stack([lax.axis_index("k"), branch, lax.axis_index("z"), lax.bitwise_xor(branch, l), l]).astype(jnp.int32)
    fw = final_weight.T

    block = lax.ppermute(out_weight.T, ("c", "k", "l"), spread_pairs())
    unit = lax.all_to_all(jnp.broadcast_to(block, (8, 192, HD)), "y", 0, 0, tiled=True).reshape(HALF, HD)

    qkv_rows, residual_rows, _ = tie(qkv[0, :, 0], residual[0, 0], block)
    packed = pack(where, qkv_rows)
    own, there, mod_half, fw_half, sides = prepare(where, residual_rows, modulation[0], fw)
    unit, there, packed = tie(unit, there, packed)
    gathered = lax.all_to_all(packed, ("y", "k"), 0, 0, tiled=True)

    units = [jnp.stack([unit, lax.ppermute(unit, ("k", "z"), CORES[0])])]
    there, _ = tie(there, units[0])
    other = lax.ppermute(there, "c", SWAP)
    units.append(lax.ppermute(units[0], ("k", "z"), CORES[1]))
    units[1], other = tie(units[1], other)
    for step in (0, 1):
        units.append(lax.ppermute(units[-1], ("k", "z"), CORES[step]))

    heads = attend(frames[0], gathered)
    rows = lax.all_to_all(heads.reshape(16, 128, HD), ("c", "y"), 0, 0, tiled=True).reshape(2, 8, 128, HD)

    keep, send = project(where, rows, units)
    came = lax.ppermute(send, "k", SWAP)
    sums, partner_sums = norm(where, keep, came, own, other, mod_half, fw_half, sides)
    came_sums = lax.ppermute(partner_sums, "c", SWAP)
    return finish(where, timestep, sums, came_sums, noisy[0].T).T[None]


def solution(mesh):
    fine = Mesh(mesh.devices.reshape(2, 8, 2, 2, 8), ("c", "y", "k", "l", "z"))
    seq, req = ("y", "k"), ("l", "z")
    return jax.shard_map(
        shards,
        mesh=fine,
        in_specs=(
            P("c", None, req, seq, None),
            P("c", req, seq, None),
            P(req, seq),
            P(),
            P("c", None, None),
            P(req, None),
            P(),
            P(req, seq, "c"),
        ),
        out_specs=P(req, seq, "c"),
        check_vma=False,
    )
```
